256 devices in a mesh: dp: 32 (over z, x), ep: 8 (over y, core).
Axes of the slice: x: 4, y: 4, z: 8, core: 2. Of those that a mesh axis runs over, the one named last changes fastest.
Arguments:
- drafts_in: bfloat16 [512, 7168], P('dp'), may hold values from -6 to 6
- cache: bfloat16 [512, 1024, 576], P(('dp', 'ep')), may hold values from -8 to 8
- queries: bfloat16 [4, 512, 64, 576], P(None, ('dp', 'ep')), may hold values from -40 to 40
- lengths: int32 [512], P(('dp', 'ep')), may hold values from 256 to 1024, as said below
- counts: int32 [32], P('dp'), may hold values from 1 to 16, as said below
- routes: int32 [4, 512, 8], P(None, 'dp'), may hold values from 0 to 31, all different within a row; in each aligned block of 16 rows (0 to 15, 16 to 31, ..., all dimensions but the last counted through in order) at most 4 rows name the same one
- norm_gain: float32 [7168], replicated, may hold values from 0.5 to 1.5
- kv_weight: bfloat16 [7168, 576], P('ep'), may hold values from -0.0625 to 0.0625
- kv_gain: float32 [512], replicated, may hold values from 0.5 to 1.5
- router: bfloat16 [7168, 32], replicated, may hold values from -0.0625 to 0.0625
- w_gate: bfloat16 [32, 7168, 1024], P('dp', None, 'ep'), may hold values from -0.0625 to 0.0625
- w_up: bfloat16 [32, 7168, 1024], P('dp', None, 'ep'), may hold values from -0.0625 to 0.0625
- w_down: bfloat16 [32, 1024, 7168], P('dp', 'ep'), may hold values from -0.1875 to 0.1875
Outputs:
- drafted: bfloat16 [4, 512, 7168], P(None, 'dp', 'ep')
- attended: bfloat16 [4, 512, 64, 512], P(None, ('dp', 'ep'))
The draws below stay inside these ranges and needn't reach their ends.
Inputs may be any that keep to these rules, and one draw needn't show every extreme that they name: `lengths`: some request slot of every draw has all 1024 positions in use. `counts`: some rank has all 16 slots live in every draw. `routes`: each row names 8 different experts; among the 16 rows of one rank at one step, at most 4 name the same expert.
All inputs are finite; a program needn't handle non-finite values.
Results may differ from the reference program's by a relative error of at most 0.025.
Values may be sent and summed in bfloat16 or wider, within the bound.
A program may use at most 128 MiB of HBM per device.

```python
import math
import jax
import jax.numpy as jnp
import numpy as np
from jax import lax

D = 7168
H = 64
LAT = 512
KD = 576
EXPH = 1024
EXPH_DEV = 128
EXPERTS = 32
TOP = 8
STEPS = 4
RMAX = 16
CTX = 1024
REQS = 512
CAP = 4


def common_cache(key):
    return jax.random.truncated_normal(key, -4.0, 4.0, (REQS, CTX, KD), jnp.float32)


def draw_cache(key, part):
    common = common_cache(key)
    return common.astype(jnp.bfloat16)


def draw_queries(key, part):
    key = jax.random.fold_in(key, 23)
    values = jax.random.truncated_normal(key, -4.0, 4.0, (STEPS, REQS, H, KD), jnp.float32)
    return values.astype(jnp.bfloat16)


def draw_lengths(key, part):
    key = jax.random.fold_in(key, 37)
    values = jax.random.randint(key, (REQS,), CTX // 4, CTX + 1)
    return values.at[0].set(CTX).astype(jnp.int32)


def draw_counts(key, part):
    key = jax.random.fold_in(key, 41)
    shift_key, forced_key = jax.random.split(key)
    ranks_total = REQS // RMAX
    shifts = jax.random.randint(shift_key, (ranks_total,), 0, 4)
    forced = jax.random.randint(forced_key, (), 0, ranks_total)
    shifts = jnp.where(jnp.arange(ranks_total) == forced, 0, shifts)
    return jnp.maximum(1, jnp.right_shift(RMAX, shifts)).astype(jnp.int32)


def block_scale(key, shape, cuts, low, high):
    level = 1.0
    for axis_at, blocks in cuts:
        heights = jax.random.uniform(jax.random.fold_in(jax.random.fold_in(key, 6), axis_at), (blocks,), jnp.float32, low / len(cuts), high / len(cuts))
        level = level * jnp.repeat(jnp.exp(heights), shape[axis_at] // blocks).reshape((-1,) + (1,) * (len(shape) - 1 - axis_at))
    return level


def assign_block(key, own, number, rows, count, top, reach, skew):
    order = jax.random.permutation(key, count)
    crowded, usual = load_shares(count, rows * top, reach, skew, True), load_shares(count, rows * top, reach, skew, False)
    places = jnp.arange(count)

    def named(sizes, turn):
        used = int((sizes > 0).sum())
        fixed = max(1, used // 4)
        moved = fixed + (places - fixed + turn * (used - fixed)) % max(1, count - fixed)
        return jnp.zeros((count,), jnp.int32).at[order[jnp.where(places < fixed, places, moved)]].set(jnp.asarray(sizes, jnp.int32))

    sizes = jnp.where(number % 4 == 0, named(crowded, number // 4), named(usual, number - number // 4 - 1))
    mixed = jax.random.permutation(jax.random.fold_in(own, 3), count)
    donor, receiver = mixed[0:count // 2 * 2:2], mixed[1:count // 2 * 2:2]
    room = jnp.minimum(sizes[donor] - 1, reach - sizes[receiver]) // 2
    room = jnp.where((donor == order[0]) | (receiver == order[0]) | (sizes[receiver] == 0), 0, jnp.maximum(room, 0))
    moved = jax.random.randint(jax.random.fold_in(own, 4), (count // 2,), 0, 1 << 20) % (room + 1)
    sizes = sizes.at[donor].add(-moved).at[receiver].add(moved)
    labels = jnp.searchsorted(jnp.cumsum(sizes), jnp.arange(rows * top), side="right").astype(jnp.int32)
    listing = labels.reshape(top, rows).T
    listing = listing[jax.random.permutation(jax.random.fold_in(own, 1), rows)]
    turn = jax.random.randint(jax.random.fold_in(own, 2), (rows, 1), 0, top)
    return jnp.take_along_axis(listing, (jnp.arange(top)[None, :] + turn) % top, axis=1)


def load_shares(number_of, total, limit, lean, full):
    loads = [(1 << 20) // math.isqrt(grade ** lean) + 1 for grade in range(1, number_of + 1)]
    largest = limit if full else min(limit, max(-(-total // number_of), total * loads[0] // sum(loads)))
    least = 1 if total - largest >= number_of - 1 else 0
    given, rest = [largest] + [least] * (number_of - 1), total - largest - least * (number_of - 1)
    while rest > 0:
        movable = [i for i in range(1, number_of) if given[i] < largest] or [i for i in range(1, number_of) if given[i] < limit]
        mass, left = sum([loads[i] for i in movable]), rest
        for i in movable:
            more = min(limit - given[i], max(1, left * loads[i] // mass), rest)
            given[i] = given[i] + more
            rest = rest - more
    return np.array(given)


def bell_draw(key, extent, deviation, limit, cuts=(), kind=jnp.bfloat16):
    drawn = jax.random.normal(key, extent, jnp.float32) * deviation
    if len(cuts) > 0:
        drawn = block_scale(key, extent, cuts, -0.22, 0.18) * drawn
    return jnp.clip(drawn, min=-limit, max=limit).astype(kind)


def setup_inputs(seed: int = 0) -> dict:
    streams_of = jax.random.split(jax.random.key(seed), 14)
    drafts_in = bell_draw(streams_of[0], (REQS, D), 1.0, 6.0, ((0, 32),))
    cache = draw_cache(jax.random.fold_in(streams_of[13], 71), 0)
    queries = draw_queries(jax.random.fold_in(streams_of[13], 71), 0)
    lengths = draw_lengths(jax.random.fold_in(streams_of[13], 71), 0)
    counts = draw_counts(jax.random.fold_in(streams_of[13], 71), 0)
    routes_keys = jax.random.split(jax.random.fold_in(streams_of[5], 1), STEPS * REQS // RMAX)
    routes_turns = jax.random.permutation(jax.random.fold_in(streams_of[5], 3), STEPS * REQS // RMAX)
    routes = jax.vmap(lambda own, number: assign_block(jax.random.fold_in(streams_of[5], 2), own, number, RMAX, EXPERTS, TOP, CAP, 1))(routes_keys, routes_turns).reshape((STEPS, REQS, TOP))
    norm_gain = jnp.clip(1.0 + 0.1 * jax.random.normal(streams_of[6], (D,), jnp.float32), 0.5, 1.5)
    kv_weight = bell_draw(streams_of[7], (D, KD), D ** -0.5, 0.0625, ((0, 8),))
    kv_gain = jnp.clip(1.0 + 0.1 * jax.random.normal(streams_of[8], (LAT,), jnp.float32), 0.5, 1.5)
    router = bell_draw(streams_of[9], (D, EXPERTS), D ** -0.5, 0.0625)
    w_gate = bell_draw(streams_of[10], (EXPERTS, D, EXPH), D ** -0.5, 0.0625, ((0, 32), (2, 8)))
    w_up = bell_draw(streams_of[11], (EXPERTS, D, EXPH), D ** -0.5, 0.0625, ((0, 32), (2, 8)))
    w_down = bell_draw(streams_of[12], (EXPERTS, EXPH, D), EXPH ** -0.5, 0.1875, ((0, 32), (1, 8)))
    return {"drafts_in": drafts_in, "cache": cache, "queries": queries, "lengths": lengths, "counts": counts, "routes": routes, "norm_gain": norm_gain, "kv_weight": kv_weight, "kv_gain": kv_gain, "router": router, "w_gate": w_gate, "w_up": w_up, "w_down": w_down}


SCALE = 0.07216878364870322
ROUTE_SCALE = 2.827
EPSILON = 1e-06
THETA = 50000.0
NEGATIVE = -1e+30

def normalize(values):
    return values * lax.rsqrt(lax.optimization_barrier(jnp.mean(values * values, axis=-1, keepdims=True)) + EPSILON)

def rounded(values):
    return lax.optimization_barrier(values.astype(jnp.bfloat16)).astype(jnp.float32)

def rotate(values, position):
    middle = values.shape[-1] // 2
    frequency = THETA ** (-jnp.arange(middle, dtype=jnp.float32) / middle)
    angles = position.astype(jnp.float32)[:, None] * frequency[None, :]
    former = values[:, :middle]
    latter = values[:, middle:]
    cosine = jnp.cos(angles)
    sine_part = jnp.sin(angles)
    return jnp.concatenate([former * cosine - latter * sine_part, former * sine_part + latter * cosine], axis=-1)

def make_key(latent_raw, kv_gain, position):
    latent = normalize(latent_raw[:, :LAT]) * kv_gain
    turned = rotate(latent_raw[:, LAT:], position)
    return jnp.concatenate([latent, turned], axis=-1).astype(jnp.bfloat16)

def attend_rank(query_now, cache_rows, filled, draft_keys, used_keys):
    query_full = query_now.astype(jnp.float32)
    cache_full = cache_rows.astype(jnp.float32)
    draft_full = draft_keys.astype(jnp.float32)
    cache_valid = jnp.arange(cache_rows.shape[1])[None, :] < filled[:, None]
    draft_valid = jnp.arange(draft_keys.shape[1]) < used_keys
    cache_scores = SCALE * jnp.einsum('thk,tpk->thp', query_full, cache_full)
    cache_scores = jnp.where(cache_valid[:, None, :], cache_scores, NEGATIVE)
    draft_scores = SCALE * jnp.einsum('thk,tjk->thj', query_full, draft_full)
    draft_scores = jnp.where(draft_valid[None, None, :], draft_scores, NEGATIVE)
    highest = jnp.maximum(lax.optimization_barrier(jnp.max(cache_scores, axis=-1)), lax.optimization_barrier(jnp.max(draft_scores, axis=-1)))
    cache_weight = jnp.where(cache_valid[:, None, :], jnp.exp(cache_scores - highest[..., None]), 0.0)
    draft_weight = jnp.where(draft_valid[None, None, :], jnp.exp(draft_scores - highest[..., None]), 0.0)
    denominator = lax.optimization_barrier(jnp.sum(cache_weight, axis=-1)) + lax.optimization_barrier(jnp.sum(draft_weight, axis=-1))
    numerator = jnp.einsum('thp,tpl->thl', rounded(cache_weight), cache_full[:, :, :LAT])
    numerator = numerator + jnp.einsum('thj,tjl->thl', rounded(draft_weight), draft_full[:, :, :LAT])
    return numerator / denominator[..., None]

def expert_block(pieces):
    inputs, gate_weight, up_weight, down_weight = pieces
    gate_value = jnp.dot(inputs, gate_weight, preferred_element_type=jnp.float32)
    up_value = jnp.dot(inputs, up_weight, preferred_element_type=jnp.float32)
    hidden_units = (jax.nn.silu(gate_value) * up_value).astype(jnp.bfloat16)
    blocks = hidden_units.shape[1] // EXPH_DEV
    split_hidden = hidden_units.reshape(hidden_units.shape[0], blocks, EXPH_DEV).astype(jnp.float32)
    split_down = down_weight.reshape(blocks, EXPH_DEV, down_weight.shape[1]).astype(jnp.float32)
    partial_value = jnp.einsum('rbf,bfd->brd', split_hidden, split_down)
    return lax.optimization_barrier(jnp.sum(rounded(partial_value), axis=0)).astype(jnp.bfloat16)

def reference(drafts_in, cache, queries, lengths, counts, routes, norm_gain, kv_weight, kv_gain, router, w_gate, w_up, w_down):
    rank_count = counts.shape[0]
    row_count = drafts_in.shape[0]
    slot_count = row_count // rank_count
    experts = router.shape[1]
    capacity = CAP
    rank_of = jnp.arange(row_count) // slot_count
    active = jnp.arange(row_count) % slot_count < counts[rank_of]
    hidden_state = drafts_in
    draft_keys = jnp.zeros((row_count, STEPS, KD), jnp.bfloat16)
    attended = []
    drafted = []
    for step_index in range(STEPS):
        hidden_wide = hidden_state.astype(jnp.float32)
        normed = (normalize(hidden_wide) * norm_gain).astype(jnp.bfloat16)
        latent_raw = jnp.dot(normed, kv_weight, preferred_element_type=jnp.float32)
        draft_keys = draft_keys.at[:, step_index, :].set(make_key(latent_raw, kv_gain, lengths + step_index))
        used_keys = step_index + 1
        outputs = lax.map(lambda pieces: attend_rank(pieces[0], pieces[1], pieces[2], pieces[3], used_keys), (queries[step_index].reshape(rank_count, slot_count, H, KD), cache.reshape(rank_count, slot_count, CTX, KD), lengths.reshape(rank_count, slot_count), draft_keys.reshape(rank_count, slot_count, STEPS, KD)))
        outputs = outputs.reshape(row_count, H, LAT)
        attended.append(jnp.where(active[:, None, None], outputs, 0.0).astype(jnp.bfloat16))
        gate_scores = jax.nn.sigmoid(jnp.dot(normed, router, preferred_element_type=jnp.float32))
        picked = routes[step_index]
        chosen = jnp.take_along_axis(gate_scores, picked, axis=1)
        weights = chosen / lax.optimization_barrier(jnp.sum(chosen, axis=1, keepdims=True)) * ROUTE_SCALE
        onehot = ((picked[:, :, None] == jnp.arange(experts)[None, None, :]) & active[:, None, None]).astype(jnp.int32)
        flattened = onehot.reshape(rank_count, slot_count * TOP, experts)
        earlier = jnp.cumsum(flattened, axis=1) - flattened
        slot_of = lax.optimization_barrier(jnp.sum(earlier * flattened, axis=-1)).reshape(row_count, TOP)
        live_pair = jnp.broadcast_to(active[:, None], (row_count, TOP))
        slot_index = jnp.where(live_pair, slot_of, capacity)
        rank_index = jnp.broadcast_to(rank_of[:, None], (row_count, TOP))
        source = jnp.broadcast_to(normed[:, None, :], (row_count, TOP, D))
        buffers = jnp.zeros((experts, rank_count, capacity, D), jnp.bfloat16)
        buffers = buffers.at[picked, rank_index, slot_index].set(source, mode='drop')
        results = lax.map(expert_block, (buffers.reshape(experts, rank_count * capacity, D), w_gate, w_up, w_down))
        results = results.reshape(experts, rank_count, capacity, D)
        fetched = results[picked, rank_index, jnp.minimum(slot_index, capacity - 1)]
        update = lax.optimization_barrier(jnp.sum(jnp.where(live_pair[..., None], weights[..., None] * fetched.astype(jnp.float32), 0.0), axis=1))
        hidden_state = (hidden_wide + update).astype(jnp.bfloat16)
        drafted.append(jnp.where(active[:, None], hidden_state, 0.0).astype(jnp.bfloat16))
    return (jnp.stack(drafted), jnp.stack(attended))
```

```python
import functools

import jax
import jax.numpy as jnp
from jax import lax
from jax.experimental import pallas as pl
from jax.experimental.pallas import tpu as pltpu
from jax.sharding import PartitionSpec as P

LAT = 512
KD = 576
TOP = 8
STEPS = 4
CAP = 4
SLOTS = 16
LANES = 128
BLOCKS = 7
SHARE = BLOCKS * LANES
MEMBERS = 8
RING = 4
EXPERTS = 32
WIDTH = SHARE * MEMBERS
UNITS = 128
HEADS = 64
CTX = 1024
REQ = 2
GROUPS = 4
ROWS = 32
HALF = ROWS // 2
OFFSETS = (0, 1, 7, 2, 6, 3, 5, 4)

SCALE = 0.07216878364870322
ROUTE_SCALE = 2.827
EPSILON = 1e-06
THETA = 50000.0
NEGATIVE = -1e30
LIFT = 2.0**60

BF16 = jnp.bfloat16
F32 = jnp.float32
MESH = pl.DeviceIdType.MESH


def iota(shape, axis):
    return lax.broadcasted_iota(jnp.int32, shape, axis)


def kernel(
    counts_ref,
    lengths_ref,
    routes_ref,
    gain_ref,
    rgain_ref,
    kv_gain_ref,
    rope_ref,
    drafts_hbm,
    cache_hbm,
    queries_hbm,
    kv_hbm,
    gate_hbm,
    up_hbm,
    down_hbm,
    drafted_ref,
    attended_ref,
    cache,
    queries,
    kv,
    wgu,
    wd,
    start,
    x_ref,
    table,
    table_t,
    perm,
    tri,
    a_out,
    a_in,
    rows_in,
    share,
    sib_in,
    opp_out,
    opp_in,
    near_out,
    near_in,
    gates,
    d_out,
    d_in,
    lat_out,
    lat_in,
    keys,
    part_o,
    part_m,
    part_l,
    load_sem,
    a_send,
    a_recv,
    b_send,
    b_near,
    b_opp,
    b_sib,
    c_send,
    c_sib,
    c_opp,
    c_near,
    d_send,
    d_recv,
    l_send,
    l_recv,
):
    dp = lax.axis_index("dp")
    ep = lax.axis_index("ep")
    z, xx = dp // RING, dp % RING
    y, core = ep // 2, ep % 2
    y_up, y_down, y_far = (y + 1) % RING, (y + RING - 1) % RING, (y + 2) % RING
    other = 1 - core
    sibling = 2 * y + other
    ep_up, ep_down = 2 * y_up + core, 2 * y_down + core
    count = counts_ref[0]

    def rank_at(i, dx, sign):
        zt = (z + 8 + sign * OFFSETS[i]) % 8
        xt = (xx + 4 + sign * dx) % 4
        return zt * RING + xt

    def load(src, dst, n):
        return pltpu.make_async_copy(src, dst, load_sem.at[n])

    loads = [
        load(
            drafts_hbm.at[:, pl.ds(pl.multiple_of(ep * SHARE, SHARE), SHARE)], start, 0
        ),
        load(kv_hbm, kv, 1),
        load(gate_hbm.at[0], wgu.at[:, 0:UNITS], 2),
        load(up_hbm.at[0], wgu.at[:, UNITS : 2 * UNITS], 3),
        load(down_hbm.at[0], wd, 4),
        load(cache_hbm, cache, 5),
        load(queries_hbm, queries, 6),
    ]
    for item in loads:
        item.start()

    barrier = pltpu.get_barrier_semaphore()
    for n in range(1, EXPERTS):
        pl.semaphore_signal(
            barrier, inc=1, device_id=((dp + n) % EXPERTS, ep), device_id_type=MESH
        )
    for n in range(1, MEMBERS):
        pl.semaphore_signal(
            barrier, inc=1, device_id=(dp, (ep + n) % MEMBERS), device_id_type=MESH
        )

    r = iota((256, 256), 0)
    c = iota((256, 256), 1)
    perm[...] = jnp.where(
        c == ((r >> 2) & 7) * 32 + (r >> 5) * 4 + (r & 3), 1.0, 0.0
    ).astype(BF16)
    r = iota((LANES, LANES), 0)
    c = iota((LANES, LANES), 1)
    tri[...] = jnp.where(((r >> 4) == (c >> 4)) & ((r & 15) < (c & 15)), 1.0, 0.0).astype(BF16)
    pr = iota((32, LANES), 0)
    pc = iota((32, LANES), 1)
    pattern = jnp.where((pr >> 2) == (pc >> 4), pr & 3, -7).astype(F32)

    def build_table(s):
        expert = iota((EXPERTS, LANES), 0)
        live = (iota((EXPERTS, LANES), 1) & 15) < count
        named = routes_ref[s]
        hit = expert == named[0:1, :]
        for k in range(1, TOP):
            hit = hit | (expert == named[k : k + 1, :])
        hit = hit & live
        before = jnp.dot(
            jnp.where(hit, 1.0, 0.0).astype(BF16), tri[...], preferred_element_type=F32
        )
        place = jnp.where(hit, before, -1.0)
        for e in range(EXPERTS):
            table[e * 32 : e * 32 + 32, :] = jnp.where(
                jnp.broadcast_to(place[e : e + 1, :], (32, LANES)) == pattern, 1.0, 0.0
            ).astype(BF16)

    def transpose_table():
        for n in range(8):
            table_t[:, n * LANES : (n + 1) * LANES] = (
                table[n * LANES : (n + 1) * LANES, :].astype(F32).T.astype(BF16)
            )

    build_table(0)
    lat_out[...] = jnp.zeros_like(lat_out)
    keys[...] = jnp.zeros_like(keys)
    loads[0].wait()
    for j in range(BLOCKS):
        x_ref[j * SLOTS : (j + 1) * SLOTS, :] = start[:, j * LANES : (j + 1) * LANES].astype(F32)
    x_ref[BLOCKS * SLOTS :, :] = jnp.zeros((SLOTS, LANES), F32)
    pl.semaphore_wait(barrier, EXPERTS - 1 + MEMBERS - 1)

    def remote(src, dst, send, recv, device):
        pltpu.make_async_remote_copy(
            src_ref=src,
            dst_ref=dst,
            send_sem=send,
            recv_sem=recv,
            device_id=device,
            device_id_type=MESH,
        ).start()

    def arrive(ref, sem):
        pltpu.make_async_copy(ref, ref, sem).wait()

    def step(s, carry):
        parity = s % 2
        xb = x_ref[...].astype(BF16)
        for i in range(8):
            zt = (z + OFFSETS[i]) % 8
            rows = table[pl.ds(pl.multiple_of(zt * LANES, LANES), LANES), :]
            picked = jnp.dot(rows, xb, preferred_element_type=F32).astype(BF16)
            a_out[pl.ds(zt * RING, RING)] = picked.reshape(RING, 32, LANES)
            for dx in range(4):
                p = i * 4 + dx
                target = rank_at(i, dx, 1)
                if p == 0:
                    pltpu.make_async_copy(
                        a_out.at[target], a_in.at[0], a_recv.at[0]
                    ).start()
                else:
                    remote(
                        a_out.at[target], a_in.at[p], a_send, a_recv.at[p // 8], (target, ep)
                    )

        def latent_send():
            @pl.when(s == 0)
            def _():
                loads[1].wait()

            xs = jnp.concatenate(
                [x_ref[j * SLOTS : (j + 1) * SLOTS, :] for j in range(BLOCKS)], axis=1
            )
            gained = (xs * gain_ref[pl.ds(ep, 1), :]).astype(BF16)
            latent = jnp.dot(gained, kv[...], preferred_element_type=F32)
            squares = jnp.broadcast_to(
                jnp.sum(xs * xs, axis=1, keepdims=True), (SLOTS, LANES)
            )
            for t in range(SLOTS):
                row = (t % 2) * 8
                for jb in range(4):
                    lat_out[t // 2, row + jb : row + jb + 1, :] = latent[
                        t : t + 1, jb * LANES : (jb + 1) * LANES
                    ]
                lat_out[t // 2, row + 4 : row + 5, 0:64] = latent[t : t + 1, LAT:KD]
                lat_out[t // 2, row + 5 : row + 6, :] = squares[t : t + 1, :]
            for n in range(1, MEMBERS):
                target = (ep + n) % MEMBERS
                remote(
                    lat_out.at[target],
                    lat_in.at[parity, ep],
                    l_send,
                    l_recv.at[parity],
                    (dp, target),
                )
            lat_in[parity, ep] = lat_out[ep]

        def latent_take():
            arrive(lat_in.at[parity, pl.ds(0, MEMBERS - 1)], l_recv.at[parity])
            total = lat_in[parity, 0]
            for n in range(1, MEMBERS):
                total = total + lat_in[parity, n]
            scale = lax.rsqrt(total[5:6, :] * (1.0 / WIDTH) + EPSILON)
            scale_second = lax.rsqrt(total[13:14, :] * (1.0 / WIDTH) + EPSILON)
            which = iota((16, LANES), 0) < 8
            raw = total * jnp.where(
                which,
                jnp.broadcast_to(scale, (16, LANES)),
                jnp.broadcast_to(scale_second, (16, LANES)),
            )
            rope = rope_ref[s]
            ahead = pltpu.roll(raw, LANES - 32, 1)
            behind = pltpu.roll(raw, 32, 1)
            for q in range(REQ):
                base = q * 8
                lat = raw[base : base + 4, :]
                mean = jnp.sum(
                    jnp.sum(lat * lat, axis=1, keepdims=True), axis=0, keepdims=True
                ) * (1.0 / LAT)
                lat = lat * lax.rsqrt(mean + EPSILON) * kv_gain_ref[...]
                for jb in range(4):
                    keys[q, jb, pl.ds(s, 1), :] = lat[jb : jb + 1, :]
                keys[q, 4, pl.ds(s, 1), :] = (
                    raw[base + 4 : base + 5, :] * rope[q : q + 1, :]
                    + ahead[base + 4 : base + 5, :] * rope[2 + q : 3 + q, :]
                    + behind[base + 4 : base + 5, :] * rope[4 + q : 5 + q, :]
                )

        def attend_cache(q):
            query = queries[s, q]
            held = cache[q]
            score = SCALE * lax.dot_general(
                query, held, (((1,), (1,)), ((), ())), preferred_element_type=F32
            )
            valid = iota((HEADS, CTX), 1) < lengths_ref[q]
            score = jnp.where(valid, score, NEGATIVE)
            top = jnp.max(score, axis=1, keepdims=True)
            prob = jnp.where(valid, jnp.exp(score - top), 0.0)
            part_m[q] = jnp.broadcast_to(top, (HEADS, LANES))
            part_l[q] = jnp.broadcast_to(jnp.sum(prob, axis=1, keepdims=True), (HEADS, LANES))
            part_o[q] = jnp.dot(prob.astype(BF16), held[:, :LAT], preferred_element_type=F32)

        def attend_draft(q):
            query = queries[s, q]
            fresh = jnp.concatenate([keys[q, jb] for jb in range(5)], axis=1).astype(BF16)
            score = SCALE * lax.dot_general(
                query, fresh[:, :KD], (((1,), (1,)), ((), ())), preferred_element_type=F32
            )
            valid = iota((HEADS, 8), 1) <= s
            score = jnp.where(valid, score, NEGATIVE)
            old_top = part_m[q][:, 0:1]
            top = jnp.maximum(jnp.max(score, axis=1, keepdims=True), old_top)
            prob = jnp.where(valid, jnp.exp(score - top), 0.0)
            shrink = jnp.exp(old_top - top)
            total = part_l[q][:, 0:1] * shrink + jnp.sum(prob, axis=1, keepdims=True)
            out = part_o[q] * shrink + jnp.dot(
                prob.astype(BF16), fresh[:, :LAT], preferred_element_type=F32
            )
            out = out / total
            own = (ep * REQ + q) < count
            attended_ref[s, q] = jnp.where(own, out, 0.0).astype(BF16)

        def gather_start(g):
            arrive(a_in.at[pl.ds(g * 8, 8)], a_recv.at[g])
            block = a_in[pl.ds(g * 8, 8)].reshape(256, LANES)
            natural = jnp.dot(perm[...], block, preferred_element_type=F32).astype(BF16)
            rows = pl.ds(g * ROWS, ROWS)
            for j in range(BLOCKS):
                rows_in[ep, rows, j * LANES : (j + 1) * LANES] = natural[
                    j * ROWS : (j + 1) * ROWS, :
                ]
            mine = rows_in.at[ep, rows]
            remote(mine, mine, b_send.at[g], b_near.at[g, 0], (dp, ep_up))
            remote(mine, mine, b_send.at[g], b_near.at[g, 1], (dp, ep_down))
            remote(mine, mine, b_send.at[g], b_sib.at[g, 0], (dp, sibling))

        def gather_pass(g):
            rows = pl.ds(g * ROWS, ROWS)
            first = pl.ds(g * ROWS, HALF)
            second = pl.ds(g * ROWS + HALF, HALF)
            got = rows_in.at[ep_down, rows]
            arrive(got, b_near.at[g, 0])
            part = rows_in.at[ep_down, first]
            remote(part, part, b_send.at[g], b_opp.at[g, 0], (dp, ep_up))
            remote(got, got, b_send.at[g], b_sib.at[g, 1], (dp, sibling))
            got = rows_in.at[ep_up, rows]
            arrive(got, b_near.at[g, 1])
            part = rows_in.at[ep_up, second]
            remote(part, part, b_send.at[g], b_opp.at[g, 1], (dp, ep_down))
            remote(got, got, b_send.at[g], b_sib.at[g, 2], (dp, sibling))

        def gather_end(g):
            far = 2 * y_far + core
            arrive(rows_in.at[far, pl.ds(g * ROWS, HALF)], b_opp.at[g, 0])
            arrive(rows_in.at[far, pl.ds(g * ROWS + HALF, HALF)], b_opp.at[g, 1])
            got = rows_in.at[far, pl.ds(g * ROWS, ROWS)]
            remote(got, got, b_send.at[g], b_sib.at[g, 3], (dp, sibling))

        def expert(g):
            rows = slice(g * ROWS, (g + 1) * ROWS)
            if g == 0:

                @pl.when(s == 0)
                def _():
                    loads[2].wait()
                    loads[3].wait()
                    loads[4].wait()

            for n in range(4):
                arrive(rows_in.at[0, pl.ds(g * ROWS, ROWS)], b_sib.at[g, n])
            total = jnp.zeros((ROWS, 2 * UNITS), F32)
            squares = jnp.zeros((ROWS, LANES), F32)
            logits = jnp.zeros((ROWS, LANES), F32)
            for e in range(MEMBERS):
                wide = rows_in[e, rows, :].astype(F32)
                gained = (wide * gain_ref[e : e + 1, :]).astype(BF16)
                total = total + jnp.dot(
                    gained, wgu[e * SHARE : (e + 1) * SHARE, :], preferred_element_type=F32
                )
                sq = wide * wide
                lg = wide * rgain_ref[e : e + 1, :]
                for j in range(BLOCKS):
                    squares = squares + sq[:, j * LANES : (j + 1) * LANES]
                    logits = logits + lg[:, j * LANES : (j + 1) * LANES]
            scale = lax.rsqrt(
                jnp.sum(squares, axis=1, keepdims=True) * (1.0 / WIDTH) + EPSILON
            )
            logit = jnp.sum(logits, axis=1, keepdims=True) * scale
            gates[g] = jnp.broadcast_to(LIFT / (1.0 + jnp.exp(-logit)), (ROWS, LANES))
            total = total * scale
            first = total[:, :UNITS]
            hidden = (first / (1.0 + jnp.exp(-first)) * total[:, UNITS:]).astype(BF16)
            for e in range(MEMBERS):
                share[g, e % 2, e // 2] = jnp.dot(
                    hidden, wd[:, e * SHARE : (e + 1) * SHARE], preferred_element_type=F32
                ).astype(BF16)
            remote(share.at[g, other], sib_in.at[g], c_send.at[g], c_sib.at[g], (dp, sibling))

        def pair(g, to):
            return share[g, core, to].astype(F32) + sib_in[g, to].astype(F32)

        def scatter_far(g):
            arrive(rows_in.at[pl.ds(0, 7), pl.ds(0, ROWS)], b_send.at[g])
            arrive(sib_in.at[g], c_sib.at[g])
            opp_out[g] = pair(g, y_far).astype(BF16)
            remote(
                opp_out.at[g, pl.ds(0, HALF)],
                opp_in.at[g, 0],
                c_send.at[g],
                c_opp.at[g, 0],
                (dp, ep_up),
            )
            remote(
                opp_out.at[g, pl.ds(HALF, HALF)],
                opp_in.at[g, 1],
                c_send.at[g],
                c_opp.at[g, 1],
                (dp, ep_down),
            )

        def scatter_near(g):
            total = pair(g, y_up)
            arrive(opp_in.at[g, 0], c_opp.at[g, 0])
            near_out[g, 0, 0:HALF, :] = (total[:HALF] + opp_in[g, 0].astype(F32)).astype(BF16)
            near_out[g, 0, HALF:ROWS, :] = total[HALF:].astype(BF16)
            remote(near_out.at[g, 0], near_in.at[g, 0], c_send.at[g], c_near.at[g, 0], (dp, ep_up))
            total = pair(g, y_down)
            arrive(opp_in.at[g, 1], c_opp.at[g, 1])
            near_out[g, 1, 0:HALF, :] = total[:HALF].astype(BF16)
            near_out[g, 1, HALF:ROWS, :] = (total[HALF:] + opp_in[g, 1].astype(F32)).astype(BF16)
            remote(
                near_out.at[g, 1], near_in.at[g, 1], c_send.at[g], c_near.at[g, 1], (dp, ep_down)
            )

        def give_back(g):
            total = pair(g, y)
            arrive(near_in.at[g, 0], c_near.at[g, 0])
            arrive(near_in.at[g, 1], c_near.at[g, 1])
            total = total + near_in[g, 0].astype(F32) + near_in[g, 1].astype(F32)
            gate = gates[g]
            parts = [
                (total[:, j * LANES : (j + 1) * LANES] * gate).astype(BF16)
                for j in range(BLOCKS)
            ]
            parts.append(gate.astype(BF16))
            block = jnp.dot(
                perm[...], jnp.concatenate(parts, axis=0), preferred_element_type=F32
            ).astype(BF16)
            d_out[pl.ds(g * 8, 8)] = block.reshape(8, 32, LANES)
            for n in range(8):
                p = g * 8 + n
                target = rank_at(p // 4, p % 4, -1)
                if p == 0:
                    pltpu.make_async_copy(d_out.at[0], d_in.at[dp], d_recv).start()
                else:
                    remote(d_out.at[p], d_in.at[dp], d_send, d_recv, (target, ep))

        latent_send()
        transpose_table()
        stages = [
            gather_start,
            gather_pass,
            gather_end,
            expert,
            scatter_far,
            scatter_near,
            give_back,
        ]
        for tick in range(GROUPS + len(stages) - 1):
            for k in (1, 2, 0, 6, 5, 4, 3):
                g = tick - k
                if 0 <= g < GROUPS:
                    stages[k](g)

        @pl.when(s == 0)
        def _():
            loads[5].wait()
            loads[6].wait()

        latent_take()
        for q in range(REQ):
            attend_cache(q)
            attend_draft(q)
        build_table(jnp.minimum(s + 1, STEPS - 1))

        arrive(d_in, d_recv)
        summed = jnp.dot(
            table_t[...], d_in[...].reshape(EXPERTS * 32, LANES), preferred_element_type=F32
        )
        weight = summed[BLOCKS * SLOTS :, :]
        alive = weight > 0.0
        factor = jnp.where(alive, ROUTE_SCALE / jnp.where(alive, weight, 1.0), 0.0)
        shown = iota((SLOTS, LANES), 0) < count
        for j in range(BLOCKS):
            rows = slice(j * SLOTS, (j + 1) * SLOTS)
            update = jnp.where(alive, summed[rows, :] * factor, 0.0)
            fresh = (x_ref[rows, :] + update).astype(BF16).astype(F32)
            x_ref[rows, :] = fresh
            drafted_ref[s, :, j * LANES : (j + 1) * LANES] = jnp.where(shown, fresh, 0.0).astype(
                BF16
            )

        arrive(a_out.at[pl.ds(0, EXPERTS - 1)], a_send)
        arrive(d_out.at[pl.ds(0, EXPERTS - 1)], d_send)
        arrive(lat_out.at[pl.ds(0, MEMBERS - 1)], l_send)
        for g in range(GROUPS):
            arrive(rows_in.at[pl.ds(0, 7), pl.ds(0, ROWS)], c_send.at[g])
        return carry

    lax.fori_loop(0, STEPS, step, 0)


def shards(
    drafts_in,
    cache,
    queries,
    lengths,
    counts,
    routes,
    norm_gain,
    kv_weight,
    kv_gain,
    router,
    w_gate,
    w_up,
    w_down,
):
    dp = lax.axis_index("dp")
    routes_t = jnp.tile(jnp.swapaxes(routes, 1, 2), (1, 1, LANES // SLOTS))
    gain = norm_gain.reshape(MEMBERS, SHARE)
    column = lax.dynamic_slice_in_dim(router, dp, 1, 1).astype(F32)
    rgain = column.reshape(MEMBERS, SHARE) * gain
    middle = (KD - LAT) // 2
    frequency = THETA ** (-jnp.arange(middle, dtype=F32) / middle)
    position = lengths[None, :] + jnp.arange(STEPS)[:, None]
    angles = position.astype(F32)[:, :, None] * frequency
    cosine, sine = jnp.cos(angles), jnp.sin(angles)
    none = jnp.zeros_like(sine)
    tail = jnp.zeros((STEPS, REQ, LANES - 2 * middle), F32)
    rope = jnp.concatenate(
        [
            jnp.concatenate([cosine, cosine, tail], axis=-1),
            jnp.concatenate([-sine, none, tail], axis=-1),
            jnp.concatenate([none, sine, tail], axis=-1),
            jnp.zeros((STEPS, REQ, LANES), F32),
        ],
        axis=1,
    )
    vmem = pl.BlockSpec(memory_space=pltpu.VMEM)
    smem = pl.BlockSpec(memory_space=pltpu.SMEM)
    hbm = pl.BlockSpec(memory_space=pl.ANY)
    dma = pltpu.SemaphoreType.DMA
    return pl.pallas_call(
        kernel,
        out_shape=(
            jax.ShapeDtypeStruct((STEPS, SLOTS, SHARE), BF16),
            jax.ShapeDtypeStruct((STEPS, REQ, HEADS, LAT), BF16),
        ),
        in_specs=[smem] * 2 + [vmem] * 5 + [hbm] * 7,
        out_specs=(vmem, vmem),
        scratch_shapes=[
            pltpu.VMEM((REQ, CTX, KD), BF16),
            pltpu.VMEM((STEPS, REQ, HEADS, KD), BF16),
            pltpu.VMEM((SHARE, KD), BF16),
            pltpu.VMEM((WIDTH, 2 * UNITS), BF16),
            pltpu.VMEM((UNITS, WIDTH), BF16),
            pltpu.VMEM((SLOTS, SHARE), BF16),
            pltpu.VMEM((LANES, LANES), F32),
            pltpu.VMEM((EXPERTS * 32, LANES), BF16),
            pltpu.VMEM((LANES, EXPERTS * 32), BF16),
            pltpu.VMEM((256, 256), BF16),
            pltpu.VMEM((LANES, LANES), BF16),
            pltpu.VMEM((EXPERTS, 32, LANES), BF16),
            pltpu.VMEM((EXPERTS, 32, LANES), BF16),
            pltpu.VMEM((MEMBERS, LANES, SHARE), BF16),
            pltpu.VMEM((GROUPS, 2, RING, ROWS, SHARE), BF16),
            pltpu.VMEM((GROUPS, RING, ROWS, SHARE), BF16),
            pltpu.VMEM((GROUPS, ROWS, SHARE), BF16),
            pltpu.VMEM((GROUPS, 2, HALF, SHARE), BF16),
            pltpu.VMEM((GROUPS, 2, ROWS, SHARE), BF16),
            pltpu.VMEM((GROUPS, 2, ROWS, SHARE), BF16),
            pltpu.VMEM((GROUPS, ROWS, LANES), F32),
            pltpu.VMEM((EXPERTS, 32, LANES), BF16),
            pltpu.VMEM((EXPERTS, 32, LANES), BF16),
            pltpu.VMEM((MEMBERS, 16, LANES), F32),
            pltpu.VMEM((2, MEMBERS, 16, LANES), F32),
            pltpu.VMEM((REQ, 5, 8, LANES), F32),
            pltpu.VMEM((REQ, HEADS, LAT), F32),
            pltpu.VMEM((REQ, HEADS, LANES), F32),
            pltpu.VMEM((REQ, HEADS, LANES), F32),
            dma((7,)),
            dma,
            dma((GROUPS,)),
            dma((GROUPS,)),
            dma((GROUPS, 2)),
            dma((GROUPS, 2)),
            dma((GROUPS, 4)),
            dma((GROUPS,)),
            dma((GROUPS,)),
            dma((GROUPS, 2)),
            dma((GROUPS, 2)),
            dma,
            dma,
            dma,
            dma((2,)),
        ],
        compiler_params=pltpu.CompilerParams(
            collective_id=0, has_side_effects=True, vmem_limit_bytes=48 * 1024 * 1024
        ),
        name="draft_steps",
    )(
        counts,
        lengths,
        routes_t,
        gain,
        rgain,
        kv_gain.reshape(LAT // LANES, LANES),
        rope,
        drafts_in,
        cache,
        queries,
        kv_weight,
        w_gate,
        w_up,
        w_down,
    )


def solution(mesh):
    return jax.shard_map(
        shards,
        mesh=mesh,
        in_specs=(
            P("dp", None),
            P(("dp", "ep"), None, None),
            P(None, ("dp", "ep"), None, None),
            P(("dp", "ep")),
            P("dp"),
            P(None, "dp", None),
            P(),
            P("ep", None),
            P(),
            P(),
            P("dp", None, "ep"),
            P("dp", None, "ep"),
            P("dp", "ep", None),
        ),
        out_specs=(P(None, "dp", "ep"), P(None, ("dp", "ep"), None, None)),
        check_vma=False,
    )
```

```python
import jax
import jax.numpy as jnp
import numpy as np
from jax import lax
from jax.experimental import pallas as pl
from jax.experimental.pallas import tpu as pltpu
from jax.sharding import PartitionSpec as P

LAT = 512
KD = 576
TOP = 8
STEPS = 4
CAP = 4
SLOTS = 16
LANES = 128
BLOCKS = 7
SHARE = BLOCKS * LANES
MEMBERS = 8
RING = 4
EXPERTS = 32
WIDTH = SHARE * MEMBERS
UNITS = 128
HEADS = 64
CTX = 1024
REQ = 2
GROUPS = 4
ROWS = 32
HALF = ROWS // 2
PLANES = 8
OFFSETS = (1, 7, 6, 3, 5, 4, 2, 0)
ACROSS = (2, 1, 3, 0)

SCALE = 0.07216878364870322
ROUTE_SCALE = 2.827
EPSILON = 1e-06
THETA = 50000.0
NEGATIVE = -1e30
LIFT = 2.0**60

ORDER = (
    ("S", 0), ("S", 1), ("S", 2), ("S", 3), ("P", 0), ("P", 1), ("E", 0), ("P", 2),
    ("E", 1), ("P", 3), ("E", 2), ("R", 0), ("E", 3), ("R", 1), ("R", 2), ("R", 3),
)

BF16 = jnp.bfloat16
F32 = jnp.float32
MESH = pl.DeviceIdType.MESH


def iota(shape, axis):
    return lax.broadcasted_iota(jnp.int32, shape, axis)


def kernel(
    counts_ref,
    lengths_ref,
    routes_hbm,
    gain_hbm,
    kv_gain_hbm,
    freq_hbm,
    drafts_hbm,
    cache_hbm,
    queries_hbm,
    kv_hbm,
    router_hbm,
    gate_hbm,
    up_hbm,
    down_hbm,
    drafted_ref,
    attended_ref,
    routes_ref,
    gain_ref,
    kv_gain_ref,
    freq_ref,
    cache,
    queries,
    kv,
    router,
    wgu,
    wd,
    start,
    x_ref,
    rgain,
    table,
    table_t,
    perm,
    a_out,
    a_in,
    rows_in,
    squares_ref,
    logits_ref,
    part_out,
    part_in,
    own_part,
    ring_out,
    ring_in,
    gates,
    d_out,
    d_in,
    lat_out,
    lat_in,
    keys,
    part_o,
    part_m,
    part_l,
    load_sem,
    wgu_sem,
    wd_sem,
    wgu_send,
    wd_send,
    a_send,
    a_recv,
    b_send,
    b_ring,
    p_send,
    p_recv,
    c_send,
    c_ring,
    d_send,
    d_recv,
    l_send,
    l_recv,
):
    dp = lax.axis_index("dp")
    ep = lax.axis_index("ep")
    z, xx = dp // RING, dp % RING
    y, core = ep // 2, ep % 2
    other = 1 - core
    sibling = 2 * y + other
    y_at = [(y + n) % RING for n in range(RING)]
    count = counts_ref[0]

    def load(src, dst, n):
        return pltpu.make_async_copy(src, dst, load_sem.at[n])

    router_base = pl.multiple_of((dp // 16) * 16, 16)
    loads = [
        load(routes_hbm, routes_ref, 0),
        load(drafts_hbm.at[:, pl.ds(pl.multiple_of(ep * SHARE, LANES), SHARE)], start, 1),
        load(gain_hbm, gain_ref, 2),
        load(kv_hbm, kv, 3),
        load(router_hbm.at[pl.ds(router_base, 16)], router, 4),
        load(kv_gain_hbm, kv_gain_ref, 5),
        load(freq_hbm, freq_ref, 6),
        load(cache_hbm, cache, 7),
        load(queries_hbm, queries, 8),
    ]
    for item in loads:
        item.start()

    def weight_views(side):
        views = []
        units = pl.ds(pl.multiple_of(core * UNITS, UNITS), UNITS)
        upper = pl.ds(pl.multiple_of((2 + core) * UNITS, UNITS), UNITS)
        for n in range(RING):
            features = pl.ds(pl.multiple_of((2 * n + side) * SHARE, LANES), SHARE)
            views.append((gate_hbm.at[0, features], wgu.at[n, :, units], wgu_sem, wgu_send))
            views.append((up_hbm.at[0, features], wgu.at[n, :, upper], wgu_sem, wgu_send))
        for n in range(RING):
            features = pl.ds(pl.multiple_of((2 * n + side) * SHARE, LANES), SHARE)
            views.append((down_hbm.at[0, :, features], wd.at[n, units], wd_sem, wd_send))
        return views

    for src, dst, sem, _ in weight_views(core):
        pltpu.make_async_copy(src, dst, sem).start()

    barrier = pltpu.get_barrier_semaphore()
    for n in range(1, EXPERTS):
        pl.semaphore_signal(
            barrier, inc=1, device_id=((dp + n) % EXPERTS, ep), device_id_type=MESH
        )
    for n in range(1, MEMBERS):
        pl.semaphore_signal(
            barrier, inc=1, device_id=(dp, (ep + n) % MEMBERS), device_id_type=MESH
        )

    pr = iota((32, LANES), 0)
    pc = iota((32, LANES), 1)
    pattern = jnp.where((pr >> 2) == (pc >> 4), pr & 3, -7).astype(F32)
    tri = jnp.where(iota((SLOTS, SLOTS), 0) < iota((SLOTS, SLOTS), 1), 1.0, 0.0).astype(BF16)
    spread = jnp.where(
        iota((SLOTS, LANES), 0) == (iota((SLOTS, LANES), 1) & 15), 1.0, 0.0
    ).astype(BF16)

    def build_table(s):
        expert = iota((EXPERTS, SLOTS), 0)
        live = iota((EXPERTS, SLOTS), 1) < count
        named = routes_ref[s]
        hit = expert == named[0:1, :]
        for k in range(1, TOP):
            hit = hit | (expert == named[k : k + 1, :])
        hit = hit & live
        before = jnp.dot(
            jnp.where(hit, 1.0, 0.0).astype(BF16), tri, preferred_element_type=F32
        )
        place = jnp.dot(
            jnp.where(hit, before, -1.0).astype(BF16), spread, preferred_element_type=F32
        )
        for e in range(EXPERTS):
            table[s, e * 32 : e * 32 + 32, :] = jnp.where(
                jnp.broadcast_to(place[e : e + 1, :], (32, LANES)) == pattern, 1.0, 0.0
            ).astype(BF16)

    def transpose_table(s):
        for n in range(8):
            table_t[s, :, n * LANES : (n + 1) * LANES] = (
                table[s, n * LANES : (n + 1) * LANES, :].astype(F32).T.astype(BF16)
            )

    def remote(src, dst, send, recv, device):
        pltpu.make_async_remote_copy(
            src_ref=src,
            dst_ref=dst,
            send_sem=send,
            recv_sem=recv,
            device_id=device,
            device_id_type=MESH,
        ).start()

    def arrive(ref, sem):
        pltpu.make_async_copy(ref, ref, sem).wait()

    def wait_slices(sem):
        arrive(rows_in.at[pl.ds(0, RING - 1), pl.ds(0, ROWS)], sem)

    def dispatch(s):
        xb = x_ref[...].astype(BF16)
        for i, dz in enumerate(OFFSETS):
            zt = (z + dz) % PLANES
            rows = table[s, pl.ds(pl.multiple_of(zt * LANES, LANES), LANES), :]
            picked = jnp.dot(rows, xb, preferred_element_type=F32).astype(BF16)
            a_out[pl.ds(zt * RING, RING)] = picked.reshape(RING, 32, LANES)
            for n, dx in enumerate(ACROSS):
                p = i * RING + n
                target = zt * RING + (xx + dx) % RING
                src, dst, sem = a_out.at[target], a_in.at[p], a_recv.at[p // PLANES]
                if dz == 0 and dx == 0:
                    pltpu.make_async_copy(src, dst, sem).start()
                else:
                    remote(src, dst, a_send, sem, (target, ep))

    def latent_send(s):
        parity = s % 2
        blocks = [x_ref[j * SLOTS : (j + 1) * SLOTS, :] for j in range(BLOCKS)]
        gained = [
            (blocks[j] * gain_ref[pl.ds(ep * BLOCKS + j, 1), :]).astype(BF16)
            for j in range(BLOCKS)
        ]
        latent = lax.dot_general(
            jnp.concatenate(gained, axis=1),
            kv[...],
            (((1,), (1,)), ((), ())),
            preferred_element_type=F32,
        )
        squares = blocks[0] * blocks[0]
        for j in range(1, BLOCKS):
            squares = squares + blocks[j] * blocks[j]
        squares = jnp.broadcast_to(jnp.sum(squares, axis=1, keepdims=True), (SLOTS, LANES))
        for t in range(SLOTS):
            row = (t % 2) * 8
            for jb in range(4):
                lat_out[t // 2, row + jb : row + jb + 1, :] = latent[
                    t : t + 1, jb * LANES : (jb + 1) * LANES
                ]
            lat_out[t // 2, row + 4 : row + 5, 0:64] = latent[t : t + 1, LAT:KD]
            lat_out[t // 2, row + 5 : row + 6, :] = squares[t : t + 1, :]
        for n in range(1, MEMBERS):
            target = (ep + n) % MEMBERS
            remote(
                lat_out.at[target], lat_in.at[parity, ep], l_send, l_recv.at[parity], (dp, target)
            )
        lat_in[parity, ep] = lat_out[ep]

    def latent_take(s):
        parity = s % 2
        arrive(lat_in.at[parity, pl.ds(0, MEMBERS - 1)], l_recv.at[parity])
        total = lat_in[parity, 0]
        for n in range(1, MEMBERS):
            total = total + lat_in[parity, n]
        scale = lax.rsqrt(total[5:6, :] * (1.0 / WIDTH) + EPSILON)
        scale_second = lax.rsqrt(total[13:14, :] * (1.0 / WIDTH) + EPSILON)
        raw = total * jnp.where(
            iota((16, LANES), 0) < 8,
            jnp.broadcast_to(scale, (16, LANES)),
            jnp.broadcast_to(scale_second, (16, LANES)),
        )
        position = jnp.where(
            iota((8, LANES), 0) == 0, lengths_ref[0] + s, lengths_ref[1] + s
        ).astype(F32)
        angle = position * freq_ref[...]
        cosine, sine = jnp.cos(angle), jnp.sin(angle)
        lane = iota((16, LANES), 1)
        ahead = jnp.where(lane < 32, -pltpu.roll(raw, LANES - 32, 1), 0.0)
        behind = jnp.where((lane >= 32) & (lane < 64), pltpu.roll(raw, 32, 1), 0.0)
        crossed = ahead + behind
        for q in range(REQ):
            base = q * 8
            lat = raw[base : base + 4, :]
            mean = jnp.sum(
                jnp.sum(lat * lat, axis=1, keepdims=True), axis=0, keepdims=True
            ) * (1.0 / LAT)
            lat = lat * lax.rsqrt(mean + EPSILON) * kv_gain_ref[...]
            for jb in range(4):
                keys[q, jb, pl.ds(s, 1), :] = lat[jb : jb + 1, :]
            keys[q, 4, pl.ds(s, 1), :] = (
                raw[base + 4 : base + 5, :] * cosine[q : q + 1, :]
                + crossed[base + 4 : base + 5, :] * sine[q : q + 1, :]
            )

    def attend_cache(q):
        query = queries[:, q].reshape(STEPS * HEADS, KD)
        score = SCALE * jnp.dot(query, cache[q], preferred_element_type=F32)
        valid = iota((STEPS * HEADS, CTX), 1) < lengths_ref[q]
        score = jnp.where(valid, score, NEGATIVE)
        top = jnp.max(score, axis=1, keepdims=True)
        prob = jnp.where(valid, jnp.exp(score - top), 0.0)
        part_m[q] = jnp.broadcast_to(top, (STEPS * HEADS, LANES))
        part_l[q] = jnp.broadcast_to(
            jnp.sum(prob, axis=1, keepdims=True), (STEPS * HEADS, LANES)
        )
        part_o[q] = lax.dot_general(
            prob.astype(BF16),
            cache[q, :LAT, :],
            (((1,), (1,)), ((), ())),
            preferred_element_type=F32,
        )

    def attend_draft(q):
        query = queries[:, q].reshape(STEPS * HEADS, KD)
        fresh = jnp.concatenate([keys[q, jb] for jb in range(5)], axis=1).astype(BF16)
        score = SCALE * lax.dot_general(
            query, fresh[:, :KD], (((1,), (1,)), ((), ())), preferred_element_type=F32
        )
        valid = iota((STEPS * HEADS, 8), 1) <= (iota((STEPS * HEADS, 8), 0) >> 6)
        score = jnp.where(valid, score, NEGATIVE)
        old_top = part_m[q][:, 0:1]
        top = jnp.maximum(jnp.max(score, axis=1, keepdims=True), old_top)
        prob = jnp.where(valid, jnp.exp(score - top), 0.0)
        shrink = jnp.exp(old_top - top)
        total = part_l[q][:, 0:1] * shrink + jnp.sum(prob, axis=1, keepdims=True)
        out = part_o[q] * shrink + jnp.dot(
            prob.astype(BF16), fresh[:, :LAT], preferred_element_type=F32
        )
        out = jnp.where((ep * REQ + q) < count, out / total, 0.0).astype(BF16)
        for n in range(STEPS):
            attended_ref[n, q] = out[n * HEADS : (n + 1) * HEADS, :]

    def absorb(g, at, first):
        e = 2 * at + core
        rows = slice(g * ROWS, (g + 1) * ROWS)
        gained = []
        for j in range(BLOCKS):
            wide = rows_in[at, rows, j * LANES : (j + 1) * LANES].astype(F32)
            gained.append((wide * gain_ref[pl.ds(e * BLOCKS + j, 1), :]).astype(BF16))
            square = wide * wide
            logit = wide * rgain[pl.ds(e * BLOCKS + j, 1), :]
            squares = square if j == 0 else squares + square
            logits = logit if j == 0 else logits + logit
        total = jnp.dot(
            jnp.concatenate(gained, axis=1), wgu[at], preferred_element_type=F32
        )
        if first:
            part_out[g, :, 0 : 4 * UNITS] = total
            squares_ref[g] = squares
            logits_ref[g] = logits
        else:
            part_out[g, :, 0 : 4 * UNITS] += total
            squares_ref[g] += squares
            logits_ref[g] += logits

    def gather_start(s, g):
        mates = pl.ds(g * PLANES, PLANES)
        arrive(a_in.at[mates], a_recv.at[g])
        block = a_in[mates].reshape(256, LANES)
        natural = jnp.dot(perm[...], block, preferred_element_type=F32).astype(BF16)
        rows = pl.ds(g * ROWS, ROWS)
        for j in range(BLOCKS):
            rows_in[y, rows, j * LANES : (j + 1) * LANES] = natural[j * ROWS : (j + 1) * ROWS, :]
        mine = rows_in.at[y, rows]
        for n in (2, 1, 3):
            remote(mine, mine, b_send.at[g], b_ring.at[g, n], (dp, 2 * y_at[n] + core))
        if g == 0:

            @pl.when(s == 0)
            def _():
                arrive(wgu, wgu_sem)

        absorb(g, y, True)

    def gather_pass(s, g):
        rows = pl.ds(g * ROWS, ROWS)
        for n in (1, 3, 2):
            at = y_at[RING - n]
            arrive(rows_in.at[at, rows], b_ring.at[g, n])
            absorb(g, at, False)
        lane = iota((ROWS, LANES), 1)
        part_out[g, :, 4 * UNITS :] = jnp.where(
            lane == 0,
            jnp.sum(squares_ref[g], axis=1, keepdims=True),
            jnp.where(lane == 1, jnp.sum(logits_ref[g], axis=1, keepdims=True), 0.0),
        )
        parity = s % 2
        remote(
            part_out.at[g], part_in.at[parity, g], p_send, p_recv.at[parity, g], (dp, sibling)
        )

    def expert(s, g):
        parity = s % 2
        arrive(part_in.at[parity, g], p_recv.at[parity, g])
        total = part_out[g] + part_in[parity, g]
        squares = total[:, 4 * UNITS : 4 * UNITS + 1]
        scale = lax.rsqrt(squares * (1.0 / WIDTH) + EPSILON)
        logit = total[:, 4 * UNITS + 1 : 4 * UNITS + 2] * scale
        gates[g] = jnp.broadcast_to(LIFT / (1.0 + jnp.exp(-logit)), (ROWS, LANES))
        first = total[:, : 2 * UNITS] * scale
        second = total[:, 2 * UNITS : 4 * UNITS] * scale
        hidden = (first / (1.0 + jnp.exp(-first)) * second).astype(BF16)
        if g == 0:

            @pl.when(s == 0)
            def _():
                arrive(wd, wd_sem)

        wait_slices(b_send.at[g])
        for n in (2, 1, 3):
            ring_out[g, n - 1] = jnp.dot(
                hidden, wd[y_at[n]], preferred_element_type=F32
            ).astype(BF16)
            remote(
                ring_out.at[g, n - 1],
                ring_in.at[g, n - 1],
                c_send.at[g],
                c_ring.at[g, n],
                (dp, 2 * y_at[n] + core),
            )
        own_part[g] = jnp.dot(hidden, wd[y], preferred_element_type=F32)

    def give_back(s, g):
        total = own_part[g]
        for n in (1, 3, 2):
            arrive(ring_in.at[g, n - 1], c_ring.at[g, n])
            total = total + ring_in[g, n - 1].astype(F32)
        gate = gates[g]
        parts = [
            (total[:, j * LANES : (j + 1) * LANES] * gate).astype(BF16) for j in range(BLOCKS)
        ]
        parts.append(gate.astype(BF16))
        block = jnp.dot(
            perm[...], jnp.concatenate(parts, axis=0), preferred_element_type=F32
        ).astype(BF16)

        d_out[pl.ds(g * PLANES, PLANES)] = block.reshape(PLANES, 32, LANES)
        for p in range(g * PLANES, (g + 1) * PLANES):
            dz, dx = OFFSETS[p // RING], ACROSS[p % RING]
            target = (z + PLANES - dz) % PLANES * RING + (xx + RING - dx) % RING
            if dz == 0 and dx == 0:
                pltpu.make_async_copy(d_out.at[p], d_in.at[dp], d_recv).start()
            else:
                remote(d_out.at[p], d_in.at[dp], d_send, d_recv, (target, ep))


    def combine(s):
        latent_take(s)

        @pl.when(s == STEPS - 1)
        def _():
            for q in range(REQ):
                attend_draft(q)

        arrive(d_in, d_recv)
        summed = jnp.dot(
            table_t[s], d_in[...].reshape(EXPERTS * 32, LANES), preferred_element_type=F32
        )
        weight = summed[BLOCKS * SLOTS :, :]
        alive = weight > 0.0
        factor = jnp.where(alive, ROUTE_SCALE / jnp.where(alive, weight, 1.0), 0.0)
        shown = iota((SLOTS, LANES), 0) < count
        for j in range(BLOCKS):
            rows = slice(j * SLOTS, (j + 1) * SLOTS)
            update = jnp.where(alive, summed[rows, :] * factor, 0.0)
            fresh = (x_ref[rows, :] + update).astype(BF16).astype(F32)
            x_ref[rows, :] = fresh
            drafted_ref[s, :, j * LANES : (j + 1) * LANES] = jnp.where(shown, fresh, 0.0).astype(
                BF16
            )
        arrive(a_out.at[pl.ds(0, EXPERTS - 1)], a_send)
        arrive(d_out.at[pl.ds(0, EXPERTS - 1)], d_send)
        arrive(lat_out.at[pl.ds(0, MEMBERS - 1)], l_send)

        @pl.when(s < STEPS - 1)
        def _():
            dispatch(s + 1)
            latent_send(s + 1)

        arrive(part_out, p_send)
        for g in range(GROUPS):
            wait_slices(c_send.at[g])

    loads[0].wait()
    build_table(0)
    lat_out[...] = jnp.zeros_like(lat_out)
    keys[...] = jnp.zeros_like(keys)
    loads[1].wait()
    for j in range(BLOCKS):
        x_ref[j * SLOTS : (j + 1) * SLOTS, :] = start[:, j * LANES : (j + 1) * LANES].astype(F32)
    x_ref[BLOCKS * SLOTS :, :] = jnp.zeros((SLOTS, LANES), F32)
    r = iota((256, 256), 0)
    c = iota((256, 256), 1)
    perm[...] = jnp.where(
        c == ((r >> 2) & 7) * 32 + (r >> 5) * 4 + (r & 3), 1.0, 0.0
    ).astype(BF16)
    pl.semaphore_wait(barrier, EXPERTS - 1 + MEMBERS - 1)
    for src, dst, sem, send in weight_views(other):
        remote(src, dst, send, sem, (dp, sibling))
    dispatch(0)
    loads[2].wait()
    loads[3].wait()
    latent_send(0)
    loads[4].wait()
    mine = iota((16, LANES), 0) == dp % 16
    for j in range(MEMBERS * BLOCKS):
        column = jnp.where(mine, router[:, j * LANES : (j + 1) * LANES].astype(F32), 0.0)
        rgain[j : j + 1, :] = jnp.sum(column, axis=0, keepdims=True) * gain_ref[j : j + 1, :]
    transpose_table(0)
    for n in range(1, STEPS):
        build_table(n)
        transpose_table(n)
    for n in range(5, 9):
        loads[n].wait()
    for q in range(REQ):
        attend_cache(q)

    events = {
        "S": gather_start,
        "P": gather_pass,
        "E": expert,
        "R": give_back,
    }

    def step(s, carry):
        for name, g in ORDER:
            events[name](s, g)
        combine(s)
        return carry

    lax.fori_loop(0, STEPS, step, 0)
    arrive(wgu.at[pl.ds(0, RING // 2)], wgu_send)
    arrive(wd.at[pl.ds(0, RING // 2)], wd_send)


def shards(
    drafts_in,
    cache,
    queries,
    lengths,
    counts,
    routes,
    norm_gain,
    kv_weight,
    kv_gain,
    router,
    w_gate,
    w_up,
    w_down,
):
    middle = (KD - LAT) // 2
    frequency = THETA ** (-np.arange(middle) / middle)
    frequency = np.concatenate([frequency, frequency, np.zeros(LANES - 2 * middle)])
    vmem = pl.BlockSpec(memory_space=pltpu.VMEM)
    smem = pl.BlockSpec(memory_space=pltpu.SMEM)
    hbm = pl.BlockSpec(memory_space=pltpu.HBM)
    dma = pltpu.SemaphoreType.DMA
    return pl.pallas_call(
        kernel,
        out_shape=(
            jax.ShapeDtypeStruct((STEPS, SLOTS, SHARE), BF16),
            jax.ShapeDtypeStruct((STEPS, REQ, HEADS, LAT), BF16),
        ),
        in_specs=[smem] * 2 + [hbm] * 12,
        out_specs=(vmem, vmem),
        scratch_shapes=[
            pltpu.VMEM((STEPS, TOP, SLOTS), jnp.int32),
            pltpu.VMEM((MEMBERS * BLOCKS, LANES), F32),
            pltpu.VMEM((LAT // LANES, LANES), F32),
            pltpu.VMEM((1, LANES), F32),
            pltpu.VMEM((REQ, KD, CTX), BF16),
            pltpu.VMEM((STEPS, REQ, HEADS, KD), BF16),
            pltpu.VMEM((KD, SHARE), BF16),
            pltpu.VMEM((16, WIDTH), BF16),
            pltpu.VMEM((RING, SHARE, 4 * UNITS), BF16),
            pltpu.VMEM((RING, 2 * UNITS, SHARE), BF16),
            pltpu.VMEM((SLOTS, SHARE), BF16),
            pltpu.VMEM((LANES, LANES), F32),
            pltpu.VMEM((MEMBERS * BLOCKS, LANES), F32),
            pltpu.VMEM((STEPS, EXPERTS * 32, LANES), BF16),
            pltpu.VMEM((STEPS, LANES, EXPERTS * 32), BF16),
            pltpu.VMEM((256, 256), BF16),
            pltpu.VMEM((EXPERTS, 32, LANES), BF16),
            pltpu.VMEM((EXPERTS, 32, LANES), BF16),
            pltpu.VMEM((RING, LANES, SHARE), BF16),
            pltpu.VMEM((GROUPS, ROWS, LANES), F32),
            pltpu.VMEM((GROUPS, ROWS, LANES), F32),
            pltpu.VMEM((GROUPS, ROWS, 5 * LANES), F32),
            pltpu.VMEM((2, GROUPS, ROWS, 5 * LANES), F32),
            pltpu.VMEM((GROUPS, ROWS, SHARE), F32),
            pltpu.VMEM((GROUPS, RING - 1, ROWS, SHARE), BF16),
            pltpu.VMEM((GROUPS, RING - 1, ROWS, SHARE), BF16),
            pltpu.VMEM((GROUPS, ROWS, LANES), F32),
            pltpu.VMEM((EXPERTS, 32, LANES), BF16),
            pltpu.VMEM((EXPERTS, 32, LANES), BF16),
            pltpu.VMEM((MEMBERS, 16, LANES), F32),
            pltpu.VMEM((2, MEMBERS, 16, LANES), F32),
            pltpu.VMEM((REQ, 5, 8, LANES), F32),
            pltpu.VMEM((REQ, STEPS * HEADS, LAT), F32),
            pltpu.VMEM((REQ, STEPS * HEADS, LANES), F32),
            pltpu.VMEM((REQ, STEPS * HEADS, LANES), F32),
            dma((9,)),
            dma,
            dma,
            dma,
            dma,
            dma,
            dma((GROUPS,)),
            dma((GROUPS,)),
            dma((GROUPS, RING)),
            dma,
            dma((2, GROUPS)),
            dma((GROUPS,)),
            dma((GROUPS, RING)),
            dma,
            dma,
            dma,
            dma((2,)),
        ],
        compiler_params=pltpu.CompilerParams(
            collective_id=0, has_side_effects=True, vmem_limit_bytes=60 * 1024 * 1024
        ),
        name="draft_steps",
    )(
        counts,
        lengths,
        jnp.swapaxes(routes, 1, 2),
        norm_gain.reshape(MEMBERS * BLOCKS, LANES),
        kv_gain.reshape(LAT // LANES, LANES),
        jnp.asarray(frequency[None, :], F32),
        drafts_in,
        jnp.swapaxes(cache, 1, 2),
        queries,
        jnp.swapaxes(kv_weight, 0, 1),
        jnp.swapaxes(router, 0, 1),
        w_gate,
        w_up,
        w_down,
    )


def solution(mesh):
    return jax.shard_map(
        shards,
        mesh=mesh,
        in_specs=(
            P("dp", None),
            P(("dp", "ep"), None, None),
            P(None, ("dp", "ep"), None, None),
            P(("dp", "ep")),
            P("dp"),
            P(None, "dp", None),
            P(),
            P("ep", None),
            P(),
            P(),
            P("dp", None, "ep"),
            P("dp", None, "ep"),
            P("dp", "ep", None),
        ),
        out_specs=(P(None, "dp", "ep"), P(None, ("dp", "ep"), None, None)),
        check_vma=False,
    )
```

```python
import jax
import jax.numpy as jnp
import numpy as np
from jax import lax
from jax.experimental import pallas as pl
from jax.experimental.pallas import tpu as pltpu
from jax.sharding import PartitionSpec as P

LAT = 512
KD = 576
TOP = 8
STEPS = 4
CAP = 4
SLOTS = 16
LANES = 128
BLOCKS = 7
SHARE = BLOCKS * LANES
MEMBERS = 8
RING = 4
EXPERTS = 32
WIDTH = SHARE * MEMBERS
UNITS = 128
HEADS = 64
CTX = 1024
REQ = 2
PLANES = 8
GROUPS = ((1, 7), (6, 3), (5, 4), (2,), (0,))
DIRECT = (False, False, False, False, True)
OFFSETS = tuple(dz for group in GROUPS for dz in group)
ACROSS = (2, 1, 3, 0)
RANKS = [4 * len(group) for group in GROUPS]
FIRST = [sum(RANKS[:g]) for g in range(len(GROUPS))]
ALONE = [g for g, direct in enumerate(DIRECT) if direct]
GATHERED = sum(ranks for ranks, direct in zip(RANKS, DIRECT) if not direct)
GROUP_OF = [g for g, ranks in enumerate(RANKS) for _ in range(ranks)]

SCALE = 0.07216878364870322
ROUTE_SCALE = 2.827
EPSILON = 1e-06
THETA = 50000.0
NEGATIVE = -1e30
LIFT = 2.0**60

ORDER = (
    ("S", 0), ("S", 1), ("S", 4), ("S", 2), ("P", 0), ("P", 4), ("S", 3), ("P", 1), ("E", 0), ("P", 2), ("E", 1), ("P", 3), ("E", 2), ("E", 3), ("E", 4), ("R", 0), ("R", 1), ("R", 2), ("R", 3),
)

BF16 = jnp.bfloat16
F32 = jnp.float32
MESH = pl.DeviceIdType.MESH


def iota(shape, axis):
    return lax.broadcasted_iota(jnp.int32, shape, axis)


def kernel(
    counts_ref,
    lengths_ref,
    routes_hbm,
    gain_hbm,
    kv_gain_hbm,
    freq_hbm,
    drafts_hbm,
    cache_hbm,
    queries_hbm,
    kv_hbm,
    router_hbm,
    gate_hbm,
    up_hbm,
    down_hbm,
    drafted_ref,
    attended_ref,
    routes_ref,
    gain_ref,
    kv_gain_ref,
    freq_ref,
    cache,
    queries,
    kv,
    router,
    wgu,
    wd,
    start,
    x_ref,
    rgain,
    table,
    table_t,
    perm,
    perm_half,
    perm_back,
    a_out,
    a_in,
    rows_in,
    squares_ref,
    logits_ref,
    part_out,
    part_in,
    own_part,
    ring_out,
    ring_in,
    gates,
    d_out,
    d_in,
    lat_out,
    lat_in,
    keys,
    part_o,
    part_m,
    part_l,
    load_sem,
    wgu_sem,
    wd_sem,
    wgu_send,
    wd_send,
    a_send,
    a_recv,
    b_send,
    b_ring,
    p_send,
    p_recv,
    c_send,
    c_ring,
    d_send,
    d_recv,
    l_send,
    l_recv,
    *direct_refs,
):
    dp = lax.axis_index("dp")
    ep = lax.axis_index("ep")
    z, xx = dp // RING, dp % RING
    y, core = ep // 2, ep % 2
    other = 1 - core
    sibling = 2 * y + other
    y_at = [(y + n) % RING for n in range(RING)]
    count = counts_ref[0]

    near = {g: direct_refs[6 * n : 6 * n + 6] for n, g in enumerate(ALONE)}

    def load(src, dst, n):
        return pltpu.make_async_copy(src, dst, load_sem.at[n])

    router_base = pl.multiple_of((dp // 16) * 16, 16)
    loads = [
        load(routes_hbm, routes_ref, 0),
        load(drafts_hbm.at[:, pl.ds(pl.multiple_of(ep * SHARE, LANES), SHARE)], start, 1),
        load(gain_hbm, gain_ref, 2),
        load(kv_hbm, kv, 3),
        load(router_hbm.at[pl.ds(router_base, 16)], router, 4),
        load(kv_gain_hbm, kv_gain_ref, 5),
        load(freq_hbm, freq_ref, 6),
        load(cache_hbm, cache, 7),
        load(queries_hbm, queries, 8),
    ]
    for item in loads:
        item.start()

    def weight_views(side):
        views = []
        units = pl.ds(pl.multiple_of(core * UNITS, UNITS), UNITS)
        upper = pl.ds(pl.multiple_of((2 + core) * UNITS, UNITS), UNITS)
        for n in range(RING):
            features = pl.ds(pl.multiple_of((2 * n + side) * SHARE, LANES), SHARE)
            views.append((gate_hbm.at[0, features], wgu.at[n, :, units], wgu_sem, wgu_send))
            views.append((up_hbm.at[0, features], wgu.at[n, :, upper], wgu_sem, wgu_send))
        for n in range(RING):
            features = pl.ds(pl.multiple_of((2 * n + side) * SHARE, LANES), SHARE)
            views.append((down_hbm.at[0, :, features], wd.at[n, units], wd_sem, wd_send))
        return views

    for src, dst, sem, _ in weight_views(core):
        pltpu.make_async_copy(src, dst, sem).start()

    barrier = pltpu.get_barrier_semaphore()
    for n in range(1, EXPERTS):
        pl.semaphore_signal(
            barrier, inc=1, device_id=((dp + n) % EXPERTS, ep), device_id_type=MESH
        )
    for n in range(1, MEMBERS):
        pl.semaphore_signal(
            barrier, inc=1, device_id=(dp, (ep + n) % MEMBERS), device_id_type=MESH
        )

    around = [
        ((z + dz) % PLANES * RING + (xx + dx) % RING, 2 * y_at[n] + core)
        for g in ALONE
        for dz in GROUPS[g]
        for dx in range(RING)
        for n in range(1, RING)
        if dz != 0 or dx != 0
    ]
    for device in around:
        pl.semaphore_signal(barrier, inc=1, device_id=device, device_id_type=MESH)

    pr = iota((32, LANES), 0)
    pc = iota((32, LANES), 1)
    pattern = jnp.where((pr >> 2) == (pc >> 4), pr & 3, -7).astype(F32)
    tri = jnp.where(iota((SLOTS, SLOTS), 0) < iota((SLOTS, SLOTS), 1), 1.0, 0.0).astype(BF16)
    spread = jnp.where(
        iota((SLOTS, LANES), 0) == (iota((SLOTS, LANES), 1) & 15), 1.0, 0.0
    ).astype(BF16)

    def build_table(s):
        expert = iota((EXPERTS, SLOTS), 0)
        live = iota((EXPERTS, SLOTS), 1) < count
        named = routes_ref[s]
        hit = expert == named[0:1, :]
        for k in range(1, TOP):
            hit = hit | (expert == named[k : k + 1, :])
        hit = hit & live
        before = jnp.dot(
            jnp.where(hit, 1.0, 0.0).astype(BF16), tri, preferred_element_type=F32
        )
        place = jnp.dot(
            jnp.where(hit, before, -1.0).astype(BF16), spread, preferred_element_type=F32
        )
        for e in range(EXPERTS):
            table[s, e * 32 : e * 32 + 32, :] = jnp.where(
                jnp.broadcast_to(place[e : e + 1, :], (32, LANES)) == pattern, 1.0, 0.0
            ).astype(BF16)

    def transpose_table(s):
        for n in range(8):
            table_t[s, :, n * LANES : (n + 1) * LANES] = (
                table[s, n * LANES : (n + 1) * LANES, :].astype(F32).T.astype(BF16)
            )

    def remote(src, dst, send, recv, device):
        pltpu.make_async_remote_copy(
            src_ref=src,
            dst_ref=dst,
            send_sem=send,
            recv_sem=recv,
            device_id=device,
            device_id_type=MESH,
        ).start()

    def arrive(ref, sem):
        pltpu.make_async_copy(ref, ref, sem).wait()

    def span(g):
        return pl.ds(FIRST[g] * CAP, RANKS[g] * CAP)

    def wait_slices(g, sem):
        arrive(rows_in.at[pl.ds(0, RING - 1), span(g)], sem.at[g])

    def dispatch(s):
        xb = x_ref[...].astype(BF16)
        for i, dz in enumerate(OFFSETS):
            zt = (z + dz) % PLANES
            rows = table[s, pl.ds(pl.multiple_of(zt * LANES, LANES), LANES), :]
            picked = jnp.dot(rows, xb, preferred_element_type=F32).astype(BF16)
            a_out[pl.ds(zt * RING, RING)] = picked.reshape(RING, 32, LANES)
            for n, dx in enumerate(ACROSS):
                p = i * RING + n
                target = zt * RING + (xx + dx) % RING
                g = GROUP_OF[p]
                src, sem = a_out.at[target], a_recv.at[g]
                if not DIRECT[g]:
                    remote(src, a_in.at[p], a_send, sem, (target, ep))
                    continue
                rows_near, _, _, send, _, _ = near[g]
                dst = rows_near.at[y * RANKS[g] + p - FIRST[g]]
                for hop in (2, 1, 3, 0):
                    if hop == 0 and dz == 0 and dx == 0:
                        pltpu.make_async_copy(src, dst, sem).start()
                    else:
                        remote(src, dst, send, sem, (target, 2 * y_at[hop] + core))

    def latent_send(s):
        parity = s % 2
        blocks = [x_ref[j * SLOTS : (j + 1) * SLOTS, :] for j in range(BLOCKS)]
        gained = [
            (blocks[j] * gain_ref[pl.ds(ep * BLOCKS + j, 1), :]).astype(BF16)
            for j in range(BLOCKS)
        ]
        latent = lax.dot_general(
            jnp.concatenate(gained, axis=1),
            kv[...],
            (((1,), (1,)), ((), ())),
            preferred_element_type=F32,
        )
        squares = blocks[0] * blocks[0]
        for j in range(1, BLOCKS):
            squares = squares + blocks[j] * blocks[j]
        squares = jnp.broadcast_to(jnp.sum(squares, axis=1, keepdims=True), (SLOTS, LANES))
        for t in range(SLOTS):
            row = (t % 2) * 8
            for jb in range(4):
                lat_out[t // 2, row + jb : row + jb + 1, :] = latent[
                    t : t + 1, jb * LANES : (jb + 1) * LANES
                ]
            lat_out[t // 2, row + 4 : row + 5, 0:64] = latent[t : t + 1, LAT:KD]
            lat_out[t // 2, row + 5 : row + 6, :] = squares[t : t + 1, :]
        for n in range(1, MEMBERS):
            target = (ep + n) % MEMBERS
            remote(
                lat_out.at[target], lat_in.at[parity, ep], l_send, l_recv.at[parity], (dp, target)
            )
        lat_in[parity, ep] = lat_out[ep]

    def latent_take(s):
        parity = s % 2
        arrive(lat_in.at[parity, pl.ds(0, MEMBERS - 1)], l_recv.at[parity])
        total = lat_in[parity, 0]
        for n in range(1, MEMBERS):
            total = total + lat_in[parity, n]
        scale = lax.rsqrt(total[5:6, :] * (1.0 / WIDTH) + EPSILON)
        scale_second = lax.rsqrt(total[13:14, :] * (1.0 / WIDTH) + EPSILON)
        raw = total * jnp.where(
            iota((16, LANES), 0) < 8,
            jnp.broadcast_to(scale, (16, LANES)),
            jnp.broadcast_to(scale_second, (16, LANES)),
        )
        position = jnp.where(
            iota((8, LANES), 0) == 0, lengths_ref[0] + s, lengths_ref[1] + s
        ).astype(F32)
        angle = position * freq_ref[...]
        cosine, sine = jnp.cos(angle), jnp.sin(angle)
        lane = iota((16, LANES), 1)
        ahead = jnp.where(lane < 32, -pltpu.roll(raw, LANES - 32, 1), 0.0)
        behind = jnp.where((lane >= 32) & (lane < 64), pltpu.roll(raw, 32, 1), 0.0)
        crossed = ahead + behind
        for q in range(REQ):
            base = q * 8
            lat = raw[base : base + 4, :]
            mean = jnp.sum(
                jnp.sum(lat * lat, axis=1, keepdims=True), axis=0, keepdims=True
            ) * (1.0 / LAT)
            lat = lat * lax.rsqrt(mean + EPSILON) * kv_gain_ref[...]
            for jb in range(4):
                keys[q, jb, pl.ds(s, 1), :] = lat[jb : jb + 1, :]
            keys[q, 4, pl.ds(s, 1), :] = (
                raw[base + 4 : base + 5, :] * cosine[q : q + 1, :]
                + crossed[base + 4 : base + 5, :] * sine[q : q + 1, :]
            )

    def attend_cache(q):
        query = queries[:, q].reshape(STEPS * HEADS, KD)
        score = SCALE * jnp.dot(query, cache[q], preferred_element_type=F32)
        valid = iota((STEPS * HEADS, CTX), 1) < lengths_ref[q]
        score = jnp.where(valid, score, NEGATIVE)
        top = jnp.max(score, axis=1, keepdims=True)
        prob = jnp.where(valid, jnp.exp(score - top), 0.0)
        part_m[q] = jnp.broadcast_to(top, (STEPS * HEADS, LANES))
        part_l[q] = jnp.broadcast_to(
            jnp.sum(prob, axis=1, keepdims=True), (STEPS * HEADS, LANES)
        )
        part_o[q] = lax.dot_general(
            prob.astype(BF16),
            cache[q, :LAT, :],
            (((1,), (1,)), ((), ())),
            preferred_element_type=F32,
        )

    def attend_draft(q):
        query = queries[:, q].reshape(STEPS * HEADS, KD)
        fresh = jnp.concatenate([keys[q, jb] for jb in range(5)], axis=1).astype(BF16)
        score = SCALE * lax.dot_general(
            query, fresh[:, :KD], (((1,), (1,)), ((), ())), preferred_element_type=F32
        )
        valid = iota((STEPS * HEADS, 8), 1) <= (iota((STEPS * HEADS, 8), 0) >> 6)
        score = jnp.where(valid, score, NEGATIVE)
        old_top = part_m[q][:, 0:1]
        top = jnp.maximum(jnp.max(score, axis=1, keepdims=True), old_top)
        prob = jnp.where(valid, jnp.exp(score - top), 0.0)
        shrink = jnp.exp(old_top - top)
        total = part_l[q][:, 0:1] * shrink + jnp.sum(prob, axis=1, keepdims=True)
        out = part_o[q] * shrink + jnp.dot(
            prob.astype(BF16), fresh[:, :LAT], preferred_element_type=F32
        )
        out = jnp.where((ep * REQ + q) < count, out / total, 0.0).astype(BF16)
        for n in range(STEPS):
            attended_ref[n, q] = out[n * HEADS : (n + 1) * HEADS, :]

    def absorb(g, at, first):
        e = 2 * at + core
        rows = span(g)
        gained = []
        for j in range(BLOCKS):
            wide = rows_in[at, rows, j * LANES : (j + 1) * LANES].astype(F32)
            gained.append((wide * gain_ref[pl.ds(e * BLOCKS + j, 1), :]).astype(BF16))
            square = wide * wide
            logit = wide * rgain[pl.ds(e * BLOCKS + j, 1), :]
            squares = square if j == 0 else squares + square
            logits = logit if j == 0 else logits + logit
        total = jnp.dot(
            jnp.concatenate(gained, axis=1), wgu[at], preferred_element_type=F32
        )
        if first:
            part_out[rows, 0 : 4 * UNITS] = total
            squares_ref[rows] = squares
            logits_ref[rows] = logits
        else:
            part_out[rows, 0 : 4 * UNITS] += total
            squares_ref[rows] += squares
            logits_ref[rows] += logits

    def gather_start(s, g):
        ranks = RANKS[g]
        rows, count_rows = span(g), ranks * CAP
        turn = perm if ranks == 8 else perm_half

        def settle(block, at):
            natural = jnp.dot(
                turn[...], block.reshape(ranks * 32, LANES), preferred_element_type=F32
            ).astype(BF16)
            for j in range(BLOCKS):
                rows_in[at, rows, j * LANES : (j + 1) * LANES] = natural[
                    j * count_rows : (j + 1) * count_rows, :
                ]

        if DIRECT[g]:
            rows_near = near[g][0]
            arrive(rows_near, a_recv.at[g])
            for at in range(RING):
                settle(rows_near[at * ranks : (at + 1) * ranks], at)
                absorb(g, at, at == 0)
            return
        mates = pl.ds(FIRST[g], ranks)
        arrive(a_in.at[mates], a_recv.at[g])
        settle(a_in[mates], y)
        mine = rows_in.at[y, rows]
        for n in (2, 1, 3):
            remote(mine, mine, b_send.at[g], b_ring.at[g, n], (dp, 2 * y_at[n] + core))
        if g == 0:

            @pl.when(s == 0)
            def _():
                arrive(wgu, wgu_sem)

        absorb(g, y, True)

    def gather_pass(s, g):
        rows = span(g)
        for n in () if DIRECT[g] else (1, 3, 2):
            at = y_at[RING - n]
            arrive(rows_in.at[at, rows], b_ring.at[g, n])
            absorb(g, at, False)
        lane = iota((RANKS[g] * CAP, LANES), 1)
        part_out[rows, 4 * UNITS :] = jnp.where(
            lane == 0,
            jnp.sum(squares_ref[rows], axis=1, keepdims=True),
            jnp.where(lane == 1, jnp.sum(logits_ref[rows], axis=1, keepdims=True), 0.0),
        )
        parity = s % 2
        remote(
            part_out.at[rows], part_in.at[parity, rows], p_send, p_recv.at[parity, g], (dp, sibling)
        )

    def expert(s, g):
        parity = s % 2
        rows = span(g)
        arrive(part_in.at[parity, rows], p_recv.at[parity, g])
        total = part_out[rows] + part_in[parity, rows]
        squares = total[:, 4 * UNITS : 4 * UNITS + 1]
        scale = lax.rsqrt(squares * (1.0 / WIDTH) + EPSILON)
        logit = total[:, 4 * UNITS + 1 : 4 * UNITS + 2] * scale
        gates[rows] = jnp.broadcast_to(LIFT / (1.0 + jnp.exp(-logit)), (RANKS[g] * CAP, LANES))
        first = total[:, : 2 * UNITS] * scale
        second = total[:, 2 * UNITS : 4 * UNITS] * scale
        hidden = (first / (1.0 + jnp.exp(-first)) * second).astype(BF16)
        if g == 0:

            @pl.when(s == 0)
            def _():
                arrive(wd, wd_sem)

        if DIRECT[g]:
            ranks = RANKS[g]
            _, out, back, _, send, recv = near[g]
            gate = gates[rows]
            for n in (2, 1, 3, 0):
                total = jnp.dot(hidden, wd[y_at[n]], preferred_element_type=F32)
                fold(g, total, gate, gate * (1.0 / RING), out.at[pl.ds(n * ranks, ranks)])
                for i in range(ranks):
                    p = FIRST[g] + i
                    target, own = home_of(p)
                    src, dst = out.at[n * ranks + i], back.at[y * ranks + i]
                    if own and n == 0:
                        pltpu.make_async_copy(src, dst, recv).start()
                    else:
                        remote(src, dst, send, recv, (target, 2 * y_at[n] + core))
            return
        wait_slices(g, b_send)
        for n in (2, 1, 3):
            ring_out[n - 1, rows] = jnp.dot(
                hidden, wd[y_at[n]], preferred_element_type=F32
            ).astype(BF16)
            remote(
                ring_out.at[n - 1, rows],
                ring_in.at[n - 1, rows],
                c_send.at[g],
                c_ring.at[g, n],
                (dp, 2 * y_at[n] + core),
            )
        own_part[rows] = jnp.dot(hidden, wd[y], preferred_element_type=F32)

    def home_of(p):
        dz, dx = OFFSETS[p // RING], ACROSS[p % RING]
        target = (z + PLANES - dz) % PLANES * RING + (xx + RING - dx) % RING
        return target, dz == 0 and dx == 0

    def fold(g, total, gate, share, out):
        ranks = RANKS[g]
        parts = [
            (total[:, j * LANES : (j + 1) * LANES] * gate).astype(BF16) for j in range(BLOCKS)
        ]
        parts.append(share.astype(BF16))
        turn = perm if ranks == 8 else perm_back
        block = jnp.dot(
            turn[...], jnp.concatenate(parts, axis=0), preferred_element_type=F32
        ).astype(BF16)
        out[...] = block.reshape(ranks, 32, LANES)

    def give_back(s, g):
        rows = span(g)
        total = own_part[rows]
        for n in (1, 3, 2):
            arrive(ring_in.at[n - 1, rows], c_ring.at[g, n])
            total = total + ring_in[n - 1, rows].astype(F32)
        gate = gates[rows]
        fold(g, total, gate, gate, d_out.at[pl.ds(FIRST[g], RANKS[g])])
        for p in range(FIRST[g], FIRST[g] + RANKS[g]):
            target, _ = home_of(p)
            remote(d_out.at[p], d_in.at[dp], d_send, d_recv, (target, ep))

    def combine(s):
        latent_take(s)

        @pl.when(s == STEPS - 1)
        def _():
            for q in range(REQ):
                attend_draft(q)

        arrive(a_out.at[pl.ds(0, GATHERED)], a_send)
        arrive(d_out.at[pl.ds(0, GATHERED)], d_send)
        arrive(lat_out.at[pl.ds(0, MEMBERS - 1)], l_send)
        arrive(part_out, p_send)
        for g in range(len(GROUPS)):
            if not DIRECT[g]:
                wait_slices(g, c_send)
        for g in ALONE:
            ranks = RANKS[g]
            rows_near, out, back, send, back_send, back_recv = near[g]
            sent = pl.ds(0, RING * ranks - (1 if 0 in GROUPS[g] else 0))
            arrive(rows_near.at[sent], send)
            arrive(out.at[sent], back_send)
            arrive(back, back_recv)
            for i in range(ranks):
                p = FIRST[g] + i
                dz, dx = OFFSETS[p // RING], ACROSS[p % RING]
                block = back[i].astype(F32)
                for n in range(1, RING):
                    block = block + back[n * ranks + i].astype(F32)
                d_in[(z + dz) % PLANES * RING + (xx + dx) % RING] = block.astype(BF16)
        arrive(d_in.at[pl.ds(0, GATHERED)], d_recv)
        summed = jnp.dot(
            table_t[s], d_in[...].reshape(EXPERTS * 32, LANES), preferred_element_type=F32
        )
        weight = summed[BLOCKS * SLOTS :, :]
        alive = weight > 0.0
        factor = jnp.where(alive, ROUTE_SCALE / jnp.where(alive, weight, 1.0), 0.0)
        for j in range(BLOCKS):
            rows = slice(j * SLOTS, (j + 1) * SLOTS)
            update = jnp.where(alive, summed[rows, :] * factor, 0.0)
            x_ref[rows, :] = (x_ref[rows, :] + update).astype(BF16).astype(F32)

        @pl.when(s < STEPS - 1)
        def _():
            dispatch(s + 1)
            latent_send(s + 1)

        shown = iota((SLOTS, LANES), 0) < count
        for j in range(BLOCKS):
            fresh = x_ref[j * SLOTS : (j + 1) * SLOTS, :]
            drafted_ref[s, :, j * LANES : (j + 1) * LANES] = jnp.where(shown, fresh, 0.0).astype(
                BF16
            )

    loads[0].wait()
    build_table(0)
    lat_out[...] = jnp.zeros_like(lat_out)
    keys[...] = jnp.zeros_like(keys)
    loads[1].wait()
    for j in range(BLOCKS):
        x_ref[j * SLOTS : (j + 1) * SLOTS, :] = start[:, j * LANES : (j + 1) * LANES].astype(F32)
    x_ref[BLOCKS * SLOTS :, :] = jnp.zeros((SLOTS, LANES), F32)
    r = iota((256, 256), 0)
    c = iota((256, 256), 1)
    perm[...] = jnp.where(
        c == ((r >> 2) & 7) * 32 + (r >> 5) * 4 + (r & 3), 1.0, 0.0
    ).astype(BF16)
    r = iota((LANES, LANES), 0)
    c = iota((LANES, LANES), 1)
    perm_half[...] = jnp.where(
        c == ((r >> 2) & 3) * 32 + (r >> 4) * 4 + (r & 3), 1.0, 0.0
    ).astype(BF16)
    perm_back[...] = jnp.where(
        r == ((c >> 2) & 3) * 32 + (c >> 4) * 4 + (c & 3), 1.0, 0.0
    ).astype(BF16)
    pl.semaphore_wait(barrier, EXPERTS - 1 + MEMBERS - 1 + len(around))
    for src, dst, sem, send in weight_views(other):
        remote(src, dst, send, sem, (dp, sibling))
    dispatch(0)
    loads[2].wait()
    loads[3].wait()
    latent_send(0)
    loads[4].wait()
    mine = iota((16, LANES), 0) == dp % 16
    for j in range(MEMBERS * BLOCKS):
        column = jnp.where(mine, router[:, j * LANES : (j + 1) * LANES].astype(F32), 0.0)
        rgain[j : j + 1, :] = jnp.sum(column, axis=0, keepdims=True) * gain_ref[j : j + 1, :]
    transpose_table(0)
    for n in range(1, STEPS):
        build_table(n)
        transpose_table(n)
    for n in range(5, 9):
        loads[n].wait()
    for q in range(REQ):
        attend_cache(q)

    events = {
        "S": gather_start,
        "P": gather_pass,
        "E": expert,
        "R": give_back,
    }

    def step(s, carry):
        for name, g in ORDER:
            events[name](s, g)
        combine(s)
        return carry

    lax.fori_loop(0, STEPS, step, 0)
    arrive(wgu.at[pl.ds(0, RING // 2)], wgu_send)
    arrive(wd.at[pl.ds(0, RING // 2)], wd_send)


def hand_over(drafted_in, attended_in, drafted_out, attended_out, *held):
    pairs = ((attended_in, held[0], attended_out), (drafted_in, held[1], drafted_out))
    into = [pltpu.make_async_copy(a, b, held[2].at[n]) for n, (a, b, _) in enumerate(pairs)]
    back = [pltpu.make_async_copy(b, c, held[3].at[n]) for n, (_, b, c) in enumerate(pairs)]
    for item in into:
        item.start()
    for first, second in zip(into, back):
        first.wait()
        second.start()
    for item in back:
        item.wait()


def shards(
    drafts_in,
    cache,
    queries,
    lengths,
    counts,
    routes,
    norm_gain,
    kv_weight,
    kv_gain,
    router,
    w_gate,
    w_up,
    w_down,
):
    middle = (KD - LAT) // 2
    frequency = THETA ** (-np.arange(middle) / middle)
    frequency = np.concatenate([frequency, frequency, np.zeros(LANES - 2 * middle)])
    vmem = pl.BlockSpec(memory_space=pltpu.VMEM)
    smem = pl.BlockSpec(memory_space=pltpu.SMEM)
    hbm = pl.BlockSpec(memory_space=pltpu.HBM)
    dma = pltpu.SemaphoreType.DMA
    results = pl.pallas_call(
        kernel,
        out_shape=(
            jax.ShapeDtypeStruct((STEPS, SLOTS, SHARE), BF16),
            jax.ShapeDtypeStruct((STEPS, REQ, HEADS, LAT), BF16),
        ),
        in_specs=[smem] * 2 + [hbm] * 12,
        out_specs=(vmem, vmem),
        scratch_shapes=[
            pltpu.VMEM((STEPS, TOP, SLOTS), jnp.int32),
            pltpu.VMEM((MEMBERS * BLOCKS, LANES), F32),
            pltpu.VMEM((LAT // LANES, LANES), F32),
            pltpu.VMEM((1, LANES), F32),
            pltpu.VMEM((REQ, KD, CTX), BF16),
            pltpu.VMEM((STEPS, REQ, HEADS, KD), BF16),
            pltpu.VMEM((KD, SHARE), BF16),
            pltpu.VMEM((16, WIDTH), BF16),
            pltpu.VMEM((RING, SHARE, 4 * UNITS), BF16),
            pltpu.VMEM((RING, 2 * UNITS, SHARE), BF16),
            pltpu.VMEM((SLOTS, SHARE), BF16),
            pltpu.VMEM((LANES, LANES), F32),
            pltpu.VMEM((MEMBERS * BLOCKS, LANES), F32),
            pltpu.VMEM((STEPS, EXPERTS * 32, LANES), BF16),
            pltpu.VMEM((STEPS, LANES, EXPERTS * 32), BF16),
            pltpu.VMEM((256, 256), BF16),
            pltpu.VMEM((LANES, LANES), BF16),
            pltpu.VMEM((LANES, LANES), BF16),
            pltpu.VMEM((EXPERTS, 32, LANES), BF16),
            pltpu.VMEM((EXPERTS, 32, LANES), BF16),
            pltpu.VMEM((RING, LANES, SHARE), BF16),
            pltpu.VMEM((LANES, LANES), F32),
            pltpu.VMEM((LANES, LANES), F32),
            pltpu.VMEM((LANES, 5 * LANES), F32),
            pltpu.VMEM((2, LANES, 5 * LANES), F32),
            pltpu.VMEM((LANES, SHARE), F32),
            pltpu.VMEM((RING - 1, LANES, SHARE), BF16),
            pltpu.VMEM((RING - 1, LANES, SHARE), BF16),
            pltpu.VMEM((LANES, LANES), F32),
            pltpu.VMEM((EXPERTS, 32, LANES), BF16),
            pltpu.VMEM((EXPERTS, 32, LANES), BF16),
            pltpu.VMEM((MEMBERS, 16, LANES), F32),
            pltpu.VMEM((2, MEMBERS, 16, LANES), F32),
            pltpu.VMEM((REQ, 5, 8, LANES), F32),
            pltpu.VMEM((REQ, STEPS * HEADS, LAT), F32),
            pltpu.VMEM((REQ, STEPS * HEADS, LANES), F32),
            pltpu.VMEM((REQ, STEPS * HEADS, LANES), F32),
            dma((9,)),
            dma,
            dma,
            dma,
            dma,
            dma,
            dma((len(GROUPS),)),
            dma((len(GROUPS),)),
            dma((len(GROUPS), RING)),
            dma,
            dma((2, len(GROUPS))),
            dma((len(GROUPS),)),
            dma((len(GROUPS), RING)),
            dma,
            dma,
            dma,
            dma((2,)),
            *[
                ref
                for g in ALONE
                for ref in (
                    pltpu.VMEM((RING * RANKS[g], 32, LANES), BF16),
                    pltpu.VMEM((RING * RANKS[g], 32, LANES), BF16),
                    pltpu.VMEM((RING * RANKS[g], 32, LANES), BF16),
                    dma,
                    dma,
                    dma,
                )
            ],
        ],
        compiler_params=pltpu.CompilerParams(
            collective_id=0, has_side_effects=True, vmem_limit_bytes=60 * 1024 * 1024
        ),
        name="draft_steps",
    )(
        counts,
        lengths,
        jnp.swapaxes(routes, 1, 2),
        norm_gain.reshape(MEMBERS * BLOCKS, LANES),
        kv_gain.reshape(LAT // LANES, LANES),
        jnp.asarray(frequency[None, :], F32),
        drafts_in,
        jnp.swapaxes(cache, 1, 2),
        queries,
        jnp.swapaxes(kv_weight, 0, 1),
        jnp.swapaxes(router, 0, 1),
        w_gate,
        w_up,
        w_down,
    )
    return pl.pallas_call(
        hand_over,
        out_shape=tuple(jax.ShapeDtypeStruct(r.shape, r.dtype) for r in results),
        in_specs=[hbm, hbm],
        out_specs=(hbm, hbm),
        scratch_shapes=[
            pltpu.VMEM(results[1].shape, BF16),
            pltpu.VMEM(results[0].shape, BF16),
            dma((2,)),
            dma((2,)),
        ],
        name="hand_over",
    )(*results)


def solution(mesh):
    return jax.shard_map(
        shards,
        mesh=mesh,
        in_specs=(
            P("dp", None),
            P(("dp", "ep"), None, None),
            P(None, ("dp", "ep"), None, None),
            P(("dp", "ep")),
            P("dp"),
            P(None, "dp", None),
            P(),
            P("ep", None),
            P(),
            P(),
            P("dp", None, "ep"),
            P("dp", None, "ep"),
            P("dp", "ep", None),
        ),
        out_specs=(P(None, "dp", "ep"), P(None, ("dp", "ep"), None, None)),
        check_vma=False,
    )
```

```python
import jax
import jax.numpy as jnp
import numpy as np
from jax import lax
from jax.experimental import pallas as pl
from jax.experimental.pallas import tpu as pltpu
from jax.sharding import PartitionSpec as P

LAT = 512
KD = 576
TOP = 8
STEPS = 4
CAP = 4
SLOTS = 16
LANES = 128
BLOCKS = 7
SHARE = BLOCKS * LANES
MEMBERS = 8
RING = 4
EXPERTS = 32
WIDTH = SHARE * MEMBERS
UNITS = 128
HEADS = 64
CTX = 1024
REQ = 2
PLANES = 8
GROUPS = ((1, 7), (6, 3), (5, 4), (2,), (0,))
DIRECT = (False, False, False, False, True)
OFFSETS = tuple(dz for group in GROUPS for dz in group)
ACROSS = (2, 1, 3, 0)
RANKS = [4 * len(group) for group in GROUPS]
FIRST = [sum(RANKS[:g]) for g in range(len(GROUPS))]
ALONE = [g for g, direct in enumerate(DIRECT) if direct]
GATHERED = sum(ranks for ranks, direct in zip(RANKS, DIRECT) if not direct)
GROUP_OF = [g for g, ranks in enumerate(RANKS) for _ in range(ranks)]

SCALE = 0.07216878364870322
ROUTE_SCALE = 2.827
EPSILON = 1e-06
THETA = 50000.0
NEGATIVE = -1e30
LIFT = 2.0**60

ORDER = (
    ("S", 0), ("S", 1), ("S", 2), ("S", 3), ("P", 0), ("S", 4), ("P", 4), ("P", 1), ("E", 0), ("P", 2), ("E", 1), ("P", 3), ("E", 2), ("E", 3), ("R", 0), ("E", 4), ("R", 1), ("R", 2), ("R", 3),
)

BF16 = jnp.bfloat16
F32 = jnp.float32
MESH = pl.DeviceIdType.MESH


def iota(shape, axis):
    return lax.broadcasted_iota(jnp.int32, shape, axis)


def kernel(
    counts_ref,
    lengths_ref,
    routes_hbm,
    gain_hbm,
    kv_gain_hbm,
    freq_hbm,
    drafts_hbm,
    cache_hbm,
    queries_hbm,
    kv_hbm,
    router_hbm,
    gate_hbm,
    up_hbm,
    down_hbm,
    drafted_ref,
    attended_ref,
    routes_ref,
    gain_ref,
    kv_gain_ref,
    freq_ref,
    cache,
    queries,
    kv,
    router,
    wgu,
    wd,
    start,
    x_ref,
    rgain,
    table,
    table_t,
    perm,
    perm_half,
    perm_back,
    a_out,
    a_in,
    rows_in,
    squares_ref,
    logits_ref,
    part_out,
    part_in,
    own_part,
    ring_out,
    ring_in,
    gates,
    d_out,
    d_in,
    lat_out,
    lat_in,
    keys,
    part_o,
    part_m,
    part_l,
    load_sem,
    wgu_sem,
    wd_sem,
    wgu_send,
    wd_send,
    a_send,
    a_recv,
    b_send,
    b_ring,
    p_send,
    p_recv,
    c_send,
    c_ring,
    d_send,
    d_recv,
    l_send,
    l_recv,
    *direct_refs,
):
    dp = lax.axis_index("dp")
    ep = lax.axis_index("ep")
    z, xx = dp // RING, dp % RING
    y, core = ep // 2, ep % 2
    other = 1 - core
    sibling = 2 * y + other
    y_at = [(y + n) % RING for n in range(RING)]
    count = counts_ref[0]

    near = {g: direct_refs[6 * n : 6 * n + 6] for n, g in enumerate(ALONE)}

    def load(src, dst, n):
        return pltpu.make_async_copy(src, dst, load_sem.at[n])

    router_base = pl.multiple_of((dp // 16) * 16, 16)
    loads = [
        load(routes_hbm, routes_ref, 0),
        load(drafts_hbm.at[:, pl.ds(pl.multiple_of(ep * SHARE, LANES), SHARE)], start, 1),
        load(gain_hbm, gain_ref, 2),
        load(kv_hbm, kv, 3),
        load(router_hbm.at[pl.ds(router_base, 16)], router, 4),
        load(kv_gain_hbm, kv_gain_ref, 5),
        load(freq_hbm, freq_ref, 6),
        load(cache_hbm, cache, 7),
        load(queries_hbm, queries, 8),
    ]
    for item in loads:
        item.start()

    def weight_views(side):
        views = []
        units = pl.ds(pl.multiple_of(core * UNITS, UNITS), UNITS)
        upper = pl.ds(pl.multiple_of((2 + core) * UNITS, UNITS), UNITS)
        for n in range(RING):
            features = pl.ds(pl.multiple_of((2 * n + side) * SHARE, LANES), SHARE)
            views.append((gate_hbm.at[0, features], wgu.at[n, :, units], wgu_sem, wgu_send))
            views.append((up_hbm.at[0, features], wgu.at[n, :, upper], wgu_sem, wgu_send))
        for n in range(RING):
            features = pl.ds(pl.multiple_of((2 * n + side) * SHARE, LANES), SHARE)
            views.append((down_hbm.at[0, :, features], wd.at[n, units], wd_sem, wd_send))
        return views

    for src, dst, sem, _ in weight_views(core):
        pltpu.make_async_copy(src, dst, sem).start()

    barrier = pltpu.get_barrier_semaphore()
    for n in range(1, EXPERTS):
        pl.semaphore_signal(
            barrier, inc=1, device_id=((dp + n) % EXPERTS, ep), device_id_type=MESH
        )
    for n in range(1, MEMBERS):
        pl.semaphore_signal(
            barrier, inc=1, device_id=(dp, (ep + n) % MEMBERS), device_id_type=MESH
        )

    around = [
        ((z + dz) % PLANES * RING + (xx + dx) % RING, 2 * y_at[n] + core)
        for g in ALONE
        for dz in GROUPS[g]
        for dx in range(RING)
        for n in range(1, RING)
        if dz != 0 or dx != 0
    ]
    for device in around:
        pl.semaphore_signal(barrier, inc=1, device_id=device, device_id_type=MESH)

    pr = iota((32, LANES), 0)
    pc = iota((32, LANES), 1)
    pattern = jnp.where((pr >> 2) == (pc >> 4), pr & 3, -7).astype(F32)
    tri = jnp.where(iota((SLOTS, SLOTS), 0) < iota((SLOTS, SLOTS), 1), 1.0, 0.0).astype(BF16)
    spread = jnp.where(
        iota((SLOTS, LANES), 0) == (iota((SLOTS, LANES), 1) & 15), 1.0, 0.0
    ).astype(BF16)

    def build_table(s):
        expert = iota((EXPERTS, SLOTS), 0)
        live = iota((EXPERTS, SLOTS), 1) < count
        named = routes_ref[s]
        hit = expert == named[0:1, :]
        for k in range(1, TOP):
            hit = hit | (expert == named[k : k + 1, :])
        hit = hit & live
        before = jnp.dot(
            jnp.where(hit, 1.0, 0.0).astype(BF16), tri, preferred_element_type=F32
        )
        place = jnp.dot(
            jnp.where(hit, before, -1.0).astype(BF16), spread, preferred_element_type=F32
        )
        for e in range(EXPERTS):
            table[s, e * 32 : e * 32 + 32, :] = jnp.where(
                jnp.broadcast_to(place[e : e + 1, :], (32, LANES)) == pattern, 1.0, 0.0
            ).astype(BF16)

    def transpose_table(s):
        for n in range(8):
            table_t[s, :, n * LANES : (n + 1) * LANES] = (
                table[s, n * LANES : (n + 1) * LANES, :].astype(F32).T.astype(BF16)
            )

    def remote(src, dst, send, recv, device):
        pltpu.make_async_remote_copy(
            src_ref=src,
            dst_ref=dst,
            send_sem=send,
            recv_sem=recv,
            device_id=device,
            device_id_type=MESH,
        ).start()

    def arrive(ref, sem):
        pltpu.make_async_copy(ref, ref, sem).wait()

    def span(g):
        return pl.ds(FIRST[g] * CAP, RANKS[g] * CAP)

    def wait_slices(g, sem):
        arrive(rows_in.at[pl.ds(0, RING - 1), span(g)], sem.at[g])

    def dispatch(s):
        xb = x_ref[...].astype(BF16)
        for i, dz in enumerate(OFFSETS):
            zt = (z + dz) % PLANES
            rows = table[s, pl.ds(pl.multiple_of(zt * LANES, LANES), LANES), :]
            picked = jnp.dot(rows, xb, preferred_element_type=F32).astype(BF16)
            a_out[pl.ds(zt * RING, RING)] = picked.reshape(RING, 32, LANES)
            for n, dx in enumerate(ACROSS):
                p = i * RING + n
                target = zt * RING + (xx + dx) % RING
                g = GROUP_OF[p]
                src, sem = a_out.at[target], a_recv.at[g]
                if not DIRECT[g]:
                    remote(src, a_in.at[p], a_send, sem, (target, ep))
                    continue
                rows_near, _, _, send, _, _ = near[g]
                dst = rows_near.at[y * RANKS[g] + p - FIRST[g]]
                for hop in (2, 1, 3, 0):
                    if hop == 0 and dz == 0 and dx == 0:
                        pltpu.make_async_copy(src, dst, sem).start()
                    else:
                        remote(src, dst, send, sem, (target, 2 * y_at[hop] + core))

    def latent_send(s):
        parity = s % 2
        blocks = [x_ref[j * SLOTS : (j + 1) * SLOTS, :] for j in range(BLOCKS)]
        gained = [
            (blocks[j] * gain_ref[pl.ds(ep * BLOCKS + j, 1), :]).astype(BF16)
            for j in range(BLOCKS)
        ]
        latent = lax.dot_general(
            jnp.concatenate(gained, axis=1),
            kv[...],
            (((1,), (1,)), ((), ())),
            preferred_element_type=F32,
        )
        squares = blocks[0] * blocks[0]
        for j in range(1, BLOCKS):
            squares = squares + blocks[j] * blocks[j]
        squares = jnp.broadcast_to(jnp.sum(squares, axis=1, keepdims=True), (SLOTS, LANES))
        for t in range(SLOTS):
            row = (t % 2) * 8
            for jb in range(4):
                lat_out[t // 2, row + jb : row + jb + 1, :] = latent[
                    t : t + 1, jb * LANES : (jb + 1) * LANES
                ]
            lat_out[t // 2, row + 4 : row + 5, 0:64] = latent[t : t + 1, LAT:KD]
            lat_out[t // 2, row + 5 : row + 6, :] = squares[t : t + 1, :]
        for n in range(1, MEMBERS):
            target = (ep + n) % MEMBERS
            remote(
                lat_out.at[target], lat_in.at[parity, ep], l_send, l_recv.at[parity], (dp, target)
            )
        lat_in[parity, ep] = lat_out[ep]

    def latent_take(s):
        parity = s % 2
        arrive(lat_in.at[parity, pl.ds(0, MEMBERS - 1)], l_recv.at[parity])
        total = lat_in[parity, 0]
        for n in range(1, MEMBERS):
            total = total + lat_in[parity, n]
        scale = lax.rsqrt(total[5:6, :] * (1.0 / WIDTH) + EPSILON)
        scale_second = lax.rsqrt(total[13:14, :] * (1.0 / WIDTH) + EPSILON)
        raw = total * jnp.where(
            iota((16, LANES), 0) < 8,
            jnp.broadcast_to(scale, (16, LANES)),
            jnp.broadcast_to(scale_second, (16, LANES)),
        )
        position = jnp.where(
            iota((8, LANES), 0) == 0, lengths_ref[0] + s, lengths_ref[1] + s
        ).astype(F32)
        angle = position * freq_ref[...]
        cosine, sine = jnp.cos(angle), jnp.sin(angle)
        lane = iota((16, LANES), 1)
        ahead = jnp.where(lane < 32, -pltpu.roll(raw, LANES - 32, 1), 0.0)
        behind = jnp.where((lane >= 32) & (lane < 64), pltpu.roll(raw, 32, 1), 0.0)
        crossed = ahead + behind
        for q in range(REQ):
            base = q * 8
            lat = raw[base : base + 4, :]
            mean = jnp.sum(
                jnp.sum(lat * lat, axis=1, keepdims=True), axis=0, keepdims=True
            ) * (1.0 / LAT)
            lat = lat * lax.rsqrt(mean + EPSILON) * kv_gain_ref[...]
            for jb in range(4):
                keys[q, jb, pl.ds(s, 1), :] = lat[jb : jb + 1, :]
            keys[q, 4, pl.ds(s, 1), :] = (
                raw[base + 4 : base + 5, :] * cosine[q : q + 1, :]
                + crossed[base + 4 : base + 5, :] * sine[q : q + 1, :]
            )

    def attend_cache(q):
        query = queries[:, q].reshape(STEPS * HEADS, KD)
        score = SCALE * jnp.dot(query, cache[q], preferred_element_type=F32)
        valid = iota((STEPS * HEADS, CTX), 1) < lengths_ref[q]
        score = jnp.where(valid, score, NEGATIVE)
        top = jnp.max(score, axis=1, keepdims=True)
        prob = jnp.where(valid, jnp.exp(score - top), 0.0)
        part_m[q] = jnp.broadcast_to(top, (STEPS * HEADS, LANES))
        part_l[q] = jnp.broadcast_to(
            jnp.sum(prob, axis=1, keepdims=True), (STEPS * HEADS, LANES)
        )
        part_o[q] = lax.dot_general(
            prob.astype(BF16),
            cache[q, :LAT, :],
            (((1,), (1,)), ((), ())),
            preferred_element_type=F32,
        )

    def attend_draft(q):
        query = queries[:, q].reshape(STEPS * HEADS, KD)
        fresh = jnp.concatenate([keys[q, jb] for jb in range(5)], axis=1).astype(BF16)
        score = SCALE * lax.dot_general(
            query, fresh[:, :KD], (((1,), (1,)), ((), ())), preferred_element_type=F32
        )
        valid = iota((STEPS * HEADS, 8), 1) <= (iota((STEPS * HEADS, 8), 0) >> 6)
        score = jnp.where(valid, score, NEGATIVE)
        old_top = part_m[q][:, 0:1]
        top = jnp.maximum(jnp.max(score, axis=1, keepdims=True), old_top)
        prob = jnp.where(valid, jnp.exp(score - top), 0.0)
        shrink = jnp.exp(old_top - top)
        total = part_l[q][:, 0:1] * shrink + jnp.sum(prob, axis=1, keepdims=True)
        out = part_o[q] * shrink + jnp.dot(
            prob.astype(BF16), fresh[:, :LAT], preferred_element_type=F32
        )
        out = jnp.where((ep * REQ + q) < count, out / total, 0.0).astype(BF16)
        for n in range(STEPS):
            attended_ref[n, q] = out[n * HEADS : (n + 1) * HEADS, :]

    def absorb(g, at, first):
        e = 2 * at + core
        rows = span(g)
        gained = []
        for j in range(BLOCKS):
            wide = rows_in[at, rows, j * LANES : (j + 1) * LANES].astype(F32)
            gained.append((wide * gain_ref[pl.ds(e * BLOCKS + j, 1), :]).astype(BF16))
            square = wide * wide
            logit = wide * rgain[pl.ds(e * BLOCKS + j, 1), :]
            squares = square if j == 0 else squares + square
            logits = logit if j == 0 else logits + logit
        total = jnp.dot(
            jnp.concatenate(gained, axis=1), wgu[at], preferred_element_type=F32
        )
        if first:
            part_out[rows, 0 : 4 * UNITS] = total
            squares_ref[rows] = squares
            logits_ref[rows] = logits
        else:
            part_out[rows, 0 : 4 * UNITS] += total
            squares_ref[rows] += squares
            logits_ref[rows] += logits

    def gather_start(s, g):
        ranks = RANKS[g]
        rows, count_rows = span(g), ranks * CAP
        turn = perm if ranks == 8 else perm_half

        def settle(block, at):
            natural = jnp.dot(
                turn[...], block.reshape(ranks * 32, LANES), preferred_element_type=F32
            ).astype(BF16)
            for j in range(BLOCKS):
                rows_in[at, rows, j * LANES : (j + 1) * LANES] = natural[
                    j * count_rows : (j + 1) * count_rows, :
                ]

        if DIRECT[g]:
            rows_near = near[g][0]
            arrive(rows_near, a_recv.at[g])
            for at in range(RING):
                settle(rows_near[at * ranks : (at + 1) * ranks], at)
                absorb(g, at, at == 0)
            return
        mates = pl.ds(FIRST[g], ranks)
        arrive(a_in.at[mates], a_recv.at[g])
        settle(a_in[mates], y)
        mine = rows_in.at[y, rows]
        for n in (2, 1, 3):
            remote(mine, mine, b_send.at[g], b_ring.at[g, n], (dp, 2 * y_at[n] + core))
        if g == 0:

            @pl.when(s == 0)
            def _():
                arrive(wgu, wgu_sem)

        absorb(g, y, True)

    def gather_pass(s, g):
        rows = span(g)
        for n in () if DIRECT[g] else (1, 3, 2):
            at = y_at[RING - n]
            arrive(rows_in.at[at, rows], b_ring.at[g, n])
            absorb(g, at, False)
        lane = iota((RANKS[g] * CAP, LANES), 1)
        part_out[rows, 4 * UNITS :] = jnp.where(
            lane == 0,
            jnp.sum(squares_ref[rows], axis=1, keepdims=True),
            jnp.where(lane == 1, jnp.sum(logits_ref[rows], axis=1, keepdims=True), 0.0),
        )
        parity = s % 2
        remote(
            part_out.at[rows], part_in.at[parity, rows], p_send, p_recv.at[parity, g], (dp, sibling)
        )

    def expert(s, g):
        parity = s % 2
        rows = span(g)
        arrive(part_in.at[parity, rows], p_recv.at[parity, g])
        total = part_out[rows] + part_in[parity, rows]
        squares = total[:, 4 * UNITS : 4 * UNITS + 1]
        scale = lax.rsqrt(squares * (1.0 / WIDTH) + EPSILON)
        logit = total[:, 4 * UNITS + 1 : 4 * UNITS + 2] * scale
        gates[rows] = jnp.broadcast_to(LIFT / (1.0 + jnp.exp(-logit)), (RANKS[g] * CAP, LANES))
        first = total[:, : 2 * UNITS] * scale
        second = total[:, 2 * UNITS : 4 * UNITS] * scale
        hidden = (first / (1.0 + jnp.exp(-first)) * second).astype(BF16)
        if g == 0:

            @pl.when(s == 0)
            def _():
                arrive(wd, wd_sem)

        if DIRECT[g]:
            ranks = RANKS[g]
            _, out, back, _, send, recv = near[g]
            gate = gates[rows]
            for n in (2, 1, 3, 0):
                total = jnp.dot(hidden, wd[y_at[n]], preferred_element_type=F32)
                fold(g, total, gate, gate * (1.0 / RING), out.at[pl.ds(n * ranks, ranks)])
                for i in range(ranks):
                    p = FIRST[g] + i
                    target, own = home_of(p)
                    src, dst = out.at[n * ranks + i], back.at[y * ranks + i]
                    if own and n == 0:
                        pltpu.make_async_copy(src, dst, recv).start()
                    else:
                        remote(src, dst, send, recv, (target, 2 * y_at[n] + core))
            return
        wait_slices(g, b_send)
        for n in (2, 1, 3):
            ring_out[n - 1, rows] = jnp.dot(
                hidden, wd[y_at[n]], preferred_element_type=F32
            ).astype(BF16)
            remote(
                ring_out.at[n - 1, rows],
                ring_in.at[n - 1, rows],
                c_send.at[g],
                c_ring.at[g, n],
                (dp, 2 * y_at[n] + core),
            )
        own_part[rows] = jnp.dot(hidden, wd[y], preferred_element_type=F32)

    def home_of(p):
        dz, dx = OFFSETS[p // RING], ACROSS[p % RING]
        target = (z + PLANES - dz) % PLANES * RING + (xx + RING - dx) % RING
        return target, dz == 0 and dx == 0

    def fold(g, total, gate, share, out):
        ranks = RANKS[g]
        parts = [
            (total[:, j * LANES : (j + 1) * LANES] * gate).astype(BF16) for j in range(BLOCKS)
        ]
        parts.append(share.astype(BF16))
        turn = perm if ranks == 8 else perm_back
        block = jnp.dot(
            turn[...], jnp.concatenate(parts, axis=0), preferred_element_type=F32
        ).astype(BF16)
        out[...] = block.reshape(ranks, 32, LANES)

    def give_back(s, g):
        rows = span(g)
        total = own_part[rows]
        for n in (1, 3, 2):
            arrive(ring_in.at[n - 1, rows], c_ring.at[g, n])
            total = total + ring_in[n - 1, rows].astype(F32)
        gate = gates[rows]
        fold(g, total, gate, gate, d_out.at[pl.ds(FIRST[g], RANKS[g])])
        for p in range(FIRST[g], FIRST[g] + RANKS[g]):
            target, _ = home_of(p)
            remote(d_out.at[p], d_in.at[dp], d_send, d_recv, (target, ep))

    def combine(s):
        latent_take(s)

        @pl.when(s == STEPS - 1)
        def _():
            for q in range(REQ):
                attend_draft(q)

        arrive(a_out.at[pl.ds(0, GATHERED)], a_send)
        arrive(d_out.at[pl.ds(0, GATHERED)], d_send)
        arrive(lat_out.at[pl.ds(0, MEMBERS - 1)], l_send)
        arrive(part_out, p_send)
        for g in range(len(GROUPS)):
            if not DIRECT[g]:
                wait_slices(g, c_send)
        for g in ALONE:
            ranks = RANKS[g]
            rows_near, out, back, send, back_send, back_recv = near[g]
            sent = pl.ds(0, RING * ranks - (1 if 0 in GROUPS[g] else 0))
            arrive(rows_near.at[sent], send)
            arrive(out.at[sent], back_send)
            arrive(back, back_recv)
            for i in range(ranks):
                p = FIRST[g] + i
                dz, dx = OFFSETS[p // RING], ACROSS[p % RING]
                block = back[i].astype(F32)
                for n in range(1, RING):
                    block = block + back[n * ranks + i].astype(F32)
                d_in[(z + dz) % PLANES * RING + (xx + dx) % RING] = block.astype(BF16)
        arrive(d_in.at[pl.ds(0, GATHERED)], d_recv)
        summed = jnp.dot(
            table_t[s], d_in[...].reshape(EXPERTS * 32, LANES), preferred_element_type=F32
        )
        weight = summed[BLOCKS * SLOTS :, :]
        alive = weight > 0.0
        factor = jnp.where(alive, ROUTE_SCALE / jnp.where(alive, weight, 1.0), 0.0)
        for j in range(BLOCKS):
            rows = slice(j * SLOTS, (j + 1) * SLOTS)
            update = jnp.where(alive, summed[rows, :] * factor, 0.0)
            x_ref[rows, :] = (x_ref[rows, :] + update).astype(BF16).astype(F32)

        @pl.when(s < STEPS - 1)
        def _():
            dispatch(s + 1)
            latent_send(s + 1)

        shown = iota((SLOTS, LANES), 0) < count
        for j in range(BLOCKS):
            fresh = x_ref[j * SLOTS : (j + 1) * SLOTS, :]
            drafted_ref[s, :, j * LANES : (j + 1) * LANES] = jnp.where(shown, fresh, 0.0).astype(
                BF16
            )

    loads[0].wait()
    build_table(0)
    lat_out[...] = jnp.zeros_like(lat_out)
    keys[...] = jnp.zeros_like(keys)
    loads[1].wait()
    for j in range(BLOCKS):
        x_ref[j * SLOTS : (j + 1) * SLOTS, :] = start[:, j * LANES : (j + 1) * LANES].astype(F32)
    x_ref[BLOCKS * SLOTS :, :] = jnp.zeros((SLOTS, LANES), F32)
    r = iota((256, 256), 0)
    c = iota((256, 256), 1)
    perm[...] = jnp.where(
        c == ((r >> 2) & 7) * 32 + (r >> 5) * 4 + (r & 3), 1.0, 0.0
    ).astype(BF16)
    r = iota((LANES, LANES), 0)
    c = iota((LANES, LANES), 1)
    perm_half[...] = jnp.where(
        c == ((r >> 2) & 3) * 32 + (r >> 4) * 4 + (r & 3), 1.0, 0.0
    ).astype(BF16)
    perm_back[...] = jnp.where(
        r == ((c >> 2) & 3) * 32 + (c >> 4) * 4 + (c & 3), 1.0, 0.0
    ).astype(BF16)
    pl.semaphore_wait(barrier, EXPERTS - 1 + MEMBERS - 1 + len(around))
    for src, dst, sem, send in weight_views(other):
        remote(src, dst, send, sem, (dp, sibling))
    dispatch(0)
    loads[2].wait()
    loads[3].wait()
    latent_send(0)
    loads[4].wait()
    mine = iota((16, LANES), 0) == dp % 16
    for j in range(MEMBERS * BLOCKS):
        column = jnp.where(mine, router[:, j * LANES : (j + 1) * LANES].astype(F32), 0.0)
        rgain[j : j + 1, :] = jnp.sum(column, axis=0, keepdims=True) * gain_ref[j : j + 1, :]
    transpose_table(0)
    for n in range(1, STEPS):
        build_table(n)
        transpose_table(n)
    for n in range(5, 9):
        loads[n].wait()
    for q in range(REQ):
        attend_cache(q)

    events = {
        "S": gather_start,
        "P": gather_pass,
        "E": expert,
        "R": give_back,
    }

    def step(s, carry):
        for name, g in ORDER:
            events[name](s, g)
        combine(s)
        return carry

    lax.fori_loop(0, STEPS, step, 0)
    arrive(wgu.at[pl.ds(0, RING // 2)], wgu_send)
    arrive(wd.at[pl.ds(0, RING // 2)], wd_send)


def hand_over(drafted_in, attended_in, drafted_out, attended_out, *held):
    pairs = ((attended_in, held[0], attended_out), (drafted_in, held[1], drafted_out))
    into = [pltpu.make_async_copy(a, b, held[2].at[n]) for n, (a, b, _) in enumerate(pairs)]
    back = [pltpu.make_async_copy(b, c, held[3].at[n]) for n, (_, b, c) in enumerate(pairs)]
    for item in into:
        item.start()
    for first, second in zip(into, back):
        first.wait()
        second.start()
    for item in back:
        item.wait()


def shards(
    drafts_in,
    cache,
    queries,
    lengths,
    counts,
    routes,
    norm_gain,
    kv_weight,
    kv_gain,
    router,
    w_gate,
    w_up,
    w_down,
):
    middle = (KD - LAT) // 2
    frequency = THETA ** (-np.arange(middle) / middle)
    frequency = np.concatenate([frequency, frequency, np.zeros(LANES - 2 * middle)])
    vmem = pl.BlockSpec(memory_space=pltpu.VMEM)
    smem = pl.BlockSpec(memory_space=pltpu.SMEM)
    hbm = pl.BlockSpec(memory_space=pltpu.HBM)
    dma = pltpu.SemaphoreType.DMA
    results = pl.pallas_call(
        kernel,
        out_shape=(
            jax.ShapeDtypeStruct((STEPS, SLOTS, SHARE), BF16),
            jax.ShapeDtypeStruct((STEPS, REQ, HEADS, LAT), BF16),
        ),
        in_specs=[smem] * 2 + [hbm] * 12,
        out_specs=(vmem, vmem),
        scratch_shapes=[
            pltpu.VMEM((STEPS, TOP, SLOTS), jnp.int32),
            pltpu.VMEM((MEMBERS * BLOCKS, LANES), F32),
            pltpu.VMEM((LAT // LANES, LANES), F32),
            pltpu.VMEM((1, LANES), F32),
            pltpu.VMEM((REQ, KD, CTX), BF16),
            pltpu.VMEM((STEPS, REQ, HEADS, KD), BF16),
            pltpu.VMEM((KD, SHARE), BF16),
            pltpu.VMEM((16, WIDTH), BF16),
            pltpu.VMEM((RING, SHARE, 4 * UNITS), BF16),
            pltpu.VMEM((RING, 2 * UNITS, SHARE), BF16),
            pltpu.VMEM((SLOTS, SHARE), BF16),
            pltpu.VMEM((LANES, LANES), F32),
            pltpu.VMEM((MEMBERS * BLOCKS, LANES), F32),
            pltpu.VMEM((STEPS, EXPERTS * 32, LANES), BF16),
            pltpu.VMEM((STEPS, LANES, EXPERTS * 32), BF16),
            pltpu.VMEM((256, 256), BF16),
            pltpu.VMEM((LANES, LANES), BF16),
            pltpu.VMEM((LANES, LANES), BF16),
            pltpu.VMEM((EXPERTS, 32, LANES), BF16),
            pltpu.VMEM((EXPERTS, 32, LANES), BF16),
            pltpu.VMEM((RING, LANES, SHARE), BF16),
            pltpu.VMEM((LANES, LANES), F32),
            pltpu.VMEM((LANES, LANES), F32),
            pltpu.VMEM((LANES, 5 * LANES), F32),
            pltpu.VMEM((2, LANES, 5 * LANES), F32),
            pltpu.VMEM((LANES, SHARE), F32),
            pltpu.VMEM((RING - 1, LANES, SHARE), BF16),
            pltpu.VMEM((RING - 1, LANES, SHARE), BF16),
            pltpu.VMEM((LANES, LANES), F32),
            pltpu.VMEM((EXPERTS, 32, LANES), BF16),
            pltpu.VMEM((EXPERTS, 32, LANES), BF16),
            pltpu.VMEM((MEMBERS, 16, LANES), F32),
            pltpu.VMEM((2, MEMBERS, 16, LANES), F32),
            pltpu.VMEM((REQ, 5, 8, LANES), F32),
            pltpu.VMEM((REQ, STEPS * HEADS, LAT), F32),
            pltpu.VMEM((REQ, STEPS * HEADS, LANES), F32),
            pltpu.VMEM((REQ, STEPS * HEADS, LANES), F32),
            dma((9,)),
            dma,
            dma,
            dma,
            dma,
            dma,
            dma((len(GROUPS),)),
            dma((len(GROUPS),)),
            dma((len(GROUPS), RING)),
            dma,
            dma((2, len(GROUPS))),
            dma((len(GROUPS),)),
            dma((len(GROUPS), RING)),
            dma,
            dma,
            dma,
            dma((2,)),
            *[
                ref
                for g in ALONE
                for ref in (
                    pltpu.VMEM((RING * RANKS[g], 32, LANES), BF16),
                    pltpu.VMEM((RING * RANKS[g], 32, LANES), BF16),
                    pltpu.VMEM((RING * RANKS[g], 32, LANES), BF16),
                    dma,
                    dma,
                    dma,
                )
            ],
        ],
        compiler_params=pltpu.CompilerParams(
            collective_id=0, has_side_effects=True, vmem_limit_bytes=60 * 1024 * 1024
        ),
        name="draft_steps",
    )(
        counts,
        lengths,
        jnp.swapaxes(routes, 1, 2),
        norm_gain.reshape(MEMBERS * BLOCKS, LANES),
        kv_gain.reshape(LAT // LANES, LANES),
        jnp.asarray(frequency[None, :], F32),
        drafts_in,
        jnp.swapaxes(cache, 1, 2),
        queries,
        jnp.swapaxes(kv_weight, 0, 1),
        jnp.swapaxes(router, 0, 1),
        w_gate,
        w_up,
        w_down,
    )
    return pl.pallas_call(
        hand_over,
        out_shape=tuple(jax.ShapeDtypeStruct(r.shape, r.dtype) for r in results),
        in_specs=[hbm, hbm],
        out_specs=(hbm, hbm),
        scratch_shapes=[
            pltpu.VMEM(results[1].shape, BF16),
            pltpu.VMEM(results[0].shape, BF16),
            dma((2,)),
            dma((2,)),
        ],
        name="hand_over",
    )(*results)


def solution(mesh):
    return jax.shard_map(
        shards,
        mesh=mesh,
        in_specs=(
            P("dp", None),
            P(("dp", "ep"), None, None),
            P(None, ("dp", "ep"), None, None),
            P(("dp", "ep")),
            P("dp"),
            P(None, "dp", None),
            P(),
            P("ep", None),
            P(),
            P(),
            P("dp", None, "ep"),
            P("dp", None, "ep"),
            P("dp", "ep", None),
        ),
        out_specs=(P(None, "dp", "ep"), P(None, ("dp", "ep"), None, None)),
        check_vma=False,
    )
```
